128 devices in a mesh: row: 8 (over y, z_hi), col: 16 (over z_lo, x, core).
Axes of the slice: x: 4, y: 4, z: 4 (z_hi: 2, z_lo: 2; z = z_hi * 2 + z_lo), core: 2. Of those that a mesh axis runs over, the one named last changes fastest.
Arguments:
- object_field: bfloat16 [2, 4096, 16384], P(None, 'row', 'col'), may hold values from -5 to 5
- probe_modes: bfloat16 [4, 2, 512, 512], replicated, may hold values from -5 to 5
- positions: int32 [128, 2], P(('row', 'col')), may hold values from 0 to 15872, as said below
- amplitudes: float32 [128, 512, 512], P(('row', 'col')), may hold values from 0.5 to 3
- live_slots: int32 [128], P(('row', 'col')), may hold values from 0 to 1, as said below
Outputs:
- object_grad: float32 [2, 4096, 16384], P(None, 'row', 'col')
- probe_grad: float32 [4, 2, 512, 512], P(None, None, ('row', 'col'))
The draws below stay inside these ranges and needn't reach their ends.
Inputs may be any that keep to these rules, and one draw needn't show every extreme that they name: `positions`: every window lies inside the object, and the top-left pixel of slot p lies in tile (r, c), rows r * 512 to (r + 1) * 512 - 1 and columns c * 1024 to (c + 1) * 1024 - 1, where p = r * 16 + c. Slot 0's window starts at pixel (0, 0) and the last slot's window ends at the object's lower right corner. `live_slots`: each slot is live or not; in every draw at least one slot is live.
All inputs are finite; a program needn't handle non-finite values.
Results may differ from the reference program's by a relative error of at most 0.0093.
Values may be sent and summed in bfloat16 or wider, within the bound.
No kernel may reach another device: no remote copies, remote signals or barrier semaphores. Data moves between devices by JAX's collectives and lax.ppermute only.
A program may use at most 128 MiB of HBM per device.

```python
import math
import jax
import jax.numpy as jnp
from jax import lax

W = 512
MODES = 4
TH = 512
TW = 1024
CAP = 1
NY = 4096
NX = 16384
POS = 128
N_COL = 16


def draw_positions(key, part):
    key = jax.random.fold_in(key, 11)
    key_row, key_col = jax.random.split(key)
    slot_index = jnp.arange(POS, dtype=jnp.int32)
    device_index = slot_index // CAP
    tile_row = device_index // N_COL
    tile_col = device_index % N_COL
    row_high = jnp.minimum(TH, NY - W - tile_row * TH + 1)
    col_high = jnp.minimum(TW, NX - W - tile_col * TW + 1)
    row_offset = jax.random.randint(key_row, (POS,), 0, row_high)
    col_offset = jax.random.randint(key_col, (POS,), 0, col_high)
    first_slot = slot_index == 0
    last_slot = slot_index == POS - 1
    row_offset = jnp.where(first_slot, 0, jnp.where(last_slot, row_high - 1, row_offset))
    col_offset = jnp.where(first_slot, 0, jnp.where(last_slot, col_high - 1, col_offset))
    return jnp.stack([tile_row * TH + row_offset, tile_col * TW + col_offset], axis=1).astype(jnp.int32)


def draw_live_slots(key, part):
    key = jax.random.fold_in(key, 23)
    key_rate, key_full, key_roll = jax.random.split(key, 3)
    device_count = POS // CAP
    device_rate = jax.random.randint(key_rate, (device_count,), 1, 10)
    full_device = jax.random.randint(key_full, (), 0, device_count)
    device_rate = jnp.where(jnp.arange(device_count) == full_device, 10, device_rate)
    roll_value = jax.random.randint(key_roll, (POS,), 0, 10)
    return (roll_value < jnp.repeat(device_rate, CAP)).astype(jnp.int32)


def levels(rng, dims, cuts, low, high):
    loudness = 1.0
    for dim, parts in cuts:
        steps = jax.random.uniform(jax.random.fold_in(jax.random.fold_in(rng, 6), dim), (parts,), jnp.float32, low / len(cuts), high / len(cuts))
        loudness = loudness * jnp.repeat(jnp.exp(steps), dims[dim] // parts).reshape((-1,) + (1,) * (len(dims) - 1 - dim))
    return loudness


def centred(stream_key, dims, width, bound, shards=(), kind=jnp.bfloat16):
    factor_of = levels(stream_key, dims, shards, -0.22, 0.18) if shards else 1.0
    values = jax.random.normal(stream_key, dims, jnp.float32) * width * factor_of
    return jnp.minimum(jnp.maximum(values, -bound), bound).astype(kind)


def setup_inputs(seed: int = 0) -> dict:
    seeds = jax.random.split(jax.random.key(seed), 6)
    return {
        "object_field": centred(seeds[0], (2, NY, NX), 0.7, 5.0, ((1, 8), (2, 16))),
        "probe_modes": centred(seeds[1], (MODES, 2, W, W), 0.7, 5.0),
        "positions": draw_positions(jax.random.fold_in(seeds[5], 71), 0),
        "amplitudes": jnp.clip(0.5 + 2.5 * jax.random.uniform(seeds[3], (POS, W, W), jnp.float32) ** levels(seeds[3], (POS, W, W), ((0, 128),), -0.2, 0.2), 0.5, 3.0),
        "live_slots": draw_live_slots(jax.random.fold_in(seeds[5], 71), 0),
    }


def tables(patch_size):
    pixel_index = jnp.arange(patch_size, dtype=jnp.int32)
    phase_step = pixel_index[:, None] * pixel_index[None, :] % patch_size
    angle_rad = phase_step.astype(jnp.float32) * (2.0 * math.pi / patch_size)
    norm_scale = 1.0 / math.sqrt(patch_size)
    cosine = (jnp.cos(angle_rad) * norm_scale).astype(jnp.bfloat16)
    sine_table = (jnp.sin(angle_rad) * norm_scale).astype(jnp.bfloat16)
    return (cosine, sine_table)

def transform(field_in, cosine, sine_table, sign_value):
    mode_count, patch_size = (field_in.shape[0], field_in.shape[-1])
    upper_band = jnp.concatenate([cosine, sign_value * sine_table], axis=1)
    lower_band = jnp.concatenate([-sign_value * sine_table, cosine], axis=1)
    left_matrix = jnp.concatenate([upper_band, lower_band], axis=0).astype(jnp.float32)
    stacked = field_in.reshape(mode_count, 2 * patch_size, patch_size).astype(jnp.float32)
    first_pass = jnp.einsum('xy,myb->mxb', left_matrix, stacked).astype(jnp.bfloat16)
    first_pass = lax.optimization_barrier(first_pass).astype(jnp.float32)
    first_pass = first_pass.reshape(mode_count, 2, patch_size, patch_size)
    with_cos = jnp.einsum('mpab,bc->mpac', first_pass, cosine.astype(jnp.float32))
    with_sin = jnp.einsum('mpab,bc->mpac', first_pass, sine_table.astype(jnp.float32))
    real_part = with_cos[:, 0] + sign_value * with_sin[:, 1]
    imag_part = with_cos[:, 1] - sign_value * with_sin[:, 0]
    return jnp.stack([real_part, imag_part], axis=1)

def exit_wave(probe_modes, patch_data):
    probe_real = probe_modes[:, 0].astype(jnp.float32)
    probe_imag = probe_modes[:, 1].astype(jnp.float32)
    patch_real = patch_data[0].astype(jnp.float32)
    patch_imag = patch_data[1].astype(jnp.float32)
    real_part = probe_real * patch_real - probe_imag * patch_imag
    imag_part = probe_real * patch_imag + probe_imag * patch_real
    return jnp.stack([real_part, imag_part], axis=1).astype(jnp.bfloat16)

def residue(far_field, amplitude, live_flag):
    intensity = lax.optimization_barrier(jnp.sum(far_field[:, 0] * far_field[:, 0] + far_field[:, 1] * far_field[:, 1], axis=0))
    modulus = jnp.sqrt(jnp.maximum(intensity, 0.25))
    weight = live_flag.astype(jnp.float32) * (1.0 - amplitude / modulus)
    return (far_field * weight[None, None]).astype(jnp.bfloat16)

def object_term(probe_modes, exit_grad):
    probe_real = probe_modes[:, 0].astype(jnp.float32)
    probe_imag = probe_modes[:, 1].astype(jnp.float32)
    grad_real = exit_grad[:, 0]
    grad_imag = exit_grad[:, 1]
    real_part = lax.optimization_barrier(jnp.sum(probe_real * grad_real + probe_imag * grad_imag, axis=0))
    imag_part = lax.optimization_barrier(jnp.sum(probe_real * grad_imag - probe_imag * grad_real, axis=0))
    return jnp.stack([real_part, imag_part], axis=0)

def probe_term(patch_data, exit_grad):
    patch_real = patch_data[0].astype(jnp.float32)
    patch_imag = patch_data[1].astype(jnp.float32)
    grad_real = exit_grad[:, 0]
    grad_imag = exit_grad[:, 1]
    real_part = patch_real * grad_real + patch_imag * grad_imag
    imag_part = patch_real * grad_imag - patch_imag * grad_real
    return jnp.stack([real_part, imag_part], axis=1)

def reference(object_field, probe_modes, positions, amplitudes, live_slots):
    patch_size = probe_modes.shape[-1]
    cosine, sine_table = tables(patch_size)

    def one_position(slot_index, carry):
        object_grad, probe_grad = carry
        zero_index = jnp.zeros((), jnp.int32)
        top_offset = positions[slot_index, 0].astype(jnp.int32)
        left_offset = positions[slot_index, 1].astype(jnp.int32)
        corner = (zero_index, top_offset, left_offset)
        patch_data = lax.dynamic_slice(object_field, corner, (2, patch_size, patch_size))
        far_field = transform(exit_wave(probe_modes, patch_data), cosine, sine_table, 1.0)
        residual_wave = residue(far_field, amplitudes[slot_index], live_slots[slot_index])
        exit_grad = transform(residual_wave, cosine, sine_table, -1.0)
        current = lax.dynamic_slice(object_grad, corner, (2, patch_size, patch_size))
        current = current + object_term(probe_modes, exit_grad)
        object_grad = lax.dynamic_update_slice(object_grad, current, corner)
        return (object_grad, probe_grad + probe_term(patch_data, exit_grad))
    start = (jnp.zeros(object_field.shape, jnp.float32), jnp.zeros(probe_modes.shape, jnp.float32))
    object_grad, probe_grad = lax.fori_loop(0, POS, one_position, start)
    return (object_grad, probe_grad)
```

```python
import functools
import math

import jax
import jax.numpy as jnp
import ml_dtypes
import numpy as np
from jax import lax
from jax.experimental import pallas as pl
from jax.experimental.pallas import tpu as pltpu
from jax.sharding import PartitionSpec as P

W = 512
Q = W // 4
AXES = ("row", "col")
MIB = 1024 * 1024
F32 = jnp.float32
BF16 = jnp.bfloat16


def block_tables():
    step = np.arange(W).astype(np.float32) * np.float32(2.0 * math.pi / W)
    scale = np.float32(1.0 / math.sqrt(W))
    cos_of = (np.cos(step) * scale).astype(ml_dtypes.bfloat16).astype(np.float32)
    sin_of = (np.sin(step) * scale).astype(ml_dtypes.bfloat16).astype(np.float32)
    short = np.arange(Q)
    forward, adjoint = [], []
    for part in range(4):
        phase = np.outer(4 * short + part, short) % W
        c, s = cos_of[phase], sin_of[phase]
        forward.append(np.block([[c, s], [-s, c]]))
        adjoint.append(np.block([[c.T, -s.T], [s.T, c.T]]))
    forward = np.stack(forward).astype(ml_dtypes.bfloat16)
    adjoint = np.stack(adjoint).astype(ml_dtypes.bfloat16)
    swap = lambda t: np.ascontiguousarray(t.transpose(0, 2, 1))
    return forward, swap(forward), adjoint, swap(adjoint)


def fold(parts, sign):
    (ar, ai), (br, bi), (cr, ci), (dr, di) = parts
    pr, pi, mr, mi = ar + cr, ai + ci, ar - cr, ai - ci
    qr, qi, nr, ni = br + dr, bi + di, br - dr, bi - di
    if sign < 0:
        nr, ni = -nr, -ni
    return (
        (pr + qr, pi + qi),
        (mr + ni, mi - nr),
        (pr - qr, pi - qi),
        (mr - ni, mi + nr),
    )


def dot(a, b):
    return jnp.dot(a, b, preferred_element_type=F32)


def amplitude_kernel(amp_ref, pick_ref, out_ref, sorted_ref):
    rows = amp_ref[...]
    high = rows.astype(BF16)
    rest = rows - high.astype(F32)
    middle = rest.astype(BF16)
    low = (rest - middle.astype(F32)).astype(BF16)
    for c in range(4):
        pick = pick_ref[:, c * Q : (c + 1) * Q]
        sorted_ref[c] = (dot(high, pick) + dot(middle, pick)) + dot(low, pick)
    for c in range(4):
        for r in range(4):
            out_ref[r * Q : (r + 1) * Q, c * Q : (c + 1) * Q] = sorted_ref[c, pl.ds(r, Q, stride=4), :]


def amplitude_parts(amp):
    source = np.arange(W)
    pick = np.zeros((W, W), ml_dtypes.bfloat16)
    pick[source, (source % 4) * Q + source // 4] = 1
    return pl.pallas_call(
        amplitude_kernel,
        out_shape=jax.ShapeDtypeStruct((W, W), F32),
        scratch_shapes=[pltpu.VMEM((4, W, Q), F32)],
        compiler_params=pltpu.CompilerParams(vmem_limit_bytes=16 * MIB),
        cost_estimate=pl.CostEstimate(flops=6 * W**3, bytes_accessed=3 * MIB, transcendentals=0),
        name="amplitude_parts",
    )(amp, jnp.asarray(pick))


def columns_kernel(start_ref, tile_ref, right_ref, out_ref):
    start = start_ref[0]
    first = start // 128
    shift = start % 128
    back = (128 - shift) % 128
    lane = lax.broadcasted_iota(jnp.int32, (32, 128), 1)
    keep = lane < 128 - shift

    def rows_step(step, carry):
        rows = pl.ds(pl.multiple_of(step * 32, 32), 32)
        for part in range(2):
            turned = []
            for k in range(5):
                block = first + k
                in_tile = pl.ds(pl.multiple_of(jnp.minimum(block, 7) * 128, 128), 128)
                in_right = pl.ds(pl.multiple_of(jnp.clip(block - 8, 0, 3) * 128, 128), 128)
                a = tile_ref[part, rows, in_tile].astype(F32)
                b = right_ref[part, rows, in_right].astype(F32)
                turned.append(pltpu.roll(jnp.where(block < 8, a, b), back, 1))
            for k in range(4):
                value = jnp.where(keep, turned[k], turned[k + 1])
                out_ref[part, rows, k * 128 : (k + 1) * 128] = value.astype(BF16)
        return carry

    lax.fori_loop(0, tile_ref.shape[1] // 32, rows_step, 0)


def window_columns(start, tile, right, name):
    rows = tile.shape[1]
    vmem = pl.BlockSpec(memory_space=pltpu.VMEM)
    return pl.pallas_call(
        columns_kernel,
        out_shape=jax.ShapeDtypeStruct((2, rows, W), BF16),
        in_specs=[pl.BlockSpec(memory_space=pltpu.SMEM), vmem, vmem],
        out_specs=vmem,
        compiler_params=pltpu.CompilerParams(vmem_limit_bytes=16 * MIB),
        cost_estimate=pl.CostEstimate(flops=4 * MIB, bytes_accessed=4 * MIB, transcendentals=0),
        name=name,
    )(start, tile, right)


def wave_kernel(
    info_ref, own_ref, below_ref, probe_ref, amp_ref, lf_ref, rf_ref, la_ref, ra_ref,
    up_ref, low_ref, send_ref, keep_ref,
    tall, patch, folded, mid, far, wide,
):
    row_start = info_ref[0]
    first_mode = info_ref[1]
    live = info_ref[2].astype(F32)

    def loop(count, body, unroll=1):
        lax.fori_loop(0, count, lambda i, c: (body(i), c)[1], 0, unroll=unroll)

    def rows16(step, base=0):
        return pl.ds(pl.multiple_of(base + step * 16, 16), 16)

    lane_blocks = [(part, k, slice(k * 128, (k + 1) * 128)) for part in range(2) for k in range(4)]

    def stack_rows(step):
        rows = rows16(step)
        for part, k, lanes in lane_blocks:
            tall[part, k, rows, :] = own_ref[part, rows, lanes].astype(F32)
            tall[part, k, rows16(step, W), :] = below_ref[part, rows, lanes].astype(F32)

    loop(W // 16, stack_rows)

    def take_rows(step):
        for part, k, lanes in lane_blocks:
            patch[part, rows16(step), lanes] = tall[part, k, pl.ds(row_start + step * 16, 16), :]

    loop(W // 16, take_rows)

    def forward(m):
        mode = lax.rem(m + first_mode, 4)

        def exit_fold(step):
            for lanes in (slice(0, 128), slice(128, 256), slice(256, 384), slice(384, 512)):
                parts = []
                for q in range(4):
                    rows = rows16(step, q * Q)
                    pr = probe_ref[mode, 0, rows, lanes].astype(F32)
                    pi = probe_ref[mode, 1, rows, lanes].astype(F32)
                    xr, xi = patch[0, rows, lanes], patch[1, rows, lanes]
                    er = (pr * xr - pi * xi).astype(BF16).astype(F32)
                    ei = (pr * xi + pi * xr).astype(BF16).astype(F32)
                    parts.append((er, ei))
                for r, (zr, zi) in enumerate(fold(parts, 1)):
                    folded[r, rows16(step), lanes] = zr.astype(BF16)
                    folded[r, rows16(step, Q), lanes] = zi.astype(BF16)

        loop(Q // 16, exit_fold)
        for r in range(4):
            mid[r] = dot(lf_ref[r], folded[r])

        def column_fold(step):
            for r in range(4):
                parts = []
                for q in range(4):
                    lanes = slice(q * 128, (q + 1) * 128)
                    yr = mid[r, rows16(step), lanes].astype(BF16).astype(F32)
                    yi = mid[r, rows16(step, Q), lanes].astype(BF16).astype(F32)
                    parts.append((yr, yi))
                for c, (wr, wi) in enumerate(fold(parts, 1)):
                    wide[c, rows16(step, r * Q), 0:128] = wr.astype(BF16)
                    wide[c, rows16(step, r * Q), 128:256] = wi.astype(BF16)

        loop(Q // 16, column_fold)
        for c in range(4):
            far[m, :, c * 256 : (c + 1) * 256] = dot(wide[c], rf_ref[c])

    loop(4, forward)

    def residual(step):
        rows = rows16(step)
        for c in range(4):
            re, im = slice(c * 256, c * 256 + 128), slice(c * 256 + 128, c * 256 + 256)
            lanes = slice(c * 128, (c + 1) * 128)
            fields = [(far[m, rows, re], far[m, rows, im]) for m in range(4)]
            intensity = sum(fr * fr + fi * fi for fr, fi in fields)
            modulus = jnp.sqrt(jnp.maximum(intensity, 0.25))
            ratio = live * (1.0 - amp_ref[rows, lanes] / modulus)
            for m, (fr, fi) in enumerate(fields):
                far[m, rows, re] = fr * ratio
                far[m, rows, im] = fi * ratio

    loop(W // 16, residual)

    up_ref[...] = jnp.zeros_like(up_ref)

    def adjoint(m, out_ref, slot):
        mode = lax.rem(m + first_mode, 4)

        def pack(step):
            for r in range(4):
                for c in range(4):
                    rows = rows16(step, r * Q)
                    lanes = slice(c * 128, (c + 1) * 128)
                    folded[r, rows16(step), lanes] = far[m, rows, c * 256 : c * 256 + 128].astype(BF16)
                    folded[r, rows16(step, Q), lanes] = far[m, rows, c * 256 + 128 : c * 256 + 256].astype(BF16)

        loop(Q // 16, pack)
        for r in range(4):
            mid[r] = dot(la_ref[r], folded[r])

        def row_unfold(step):
            for c in range(4):
                lanes = slice(c * 128, (c + 1) * 128)
                parts = [(mid[r, rows16(step), lanes], mid[r, rows16(step, Q), lanes]) for r in range(4)]
                for q, (yr, yi) in enumerate(fold(parts, -1)):
                    wide[c, rows16(step, q * Q), 0:128] = yr.astype(BF16)
                    wide[c, rows16(step, q * Q), 128:256] = yi.astype(BF16)

        loop(Q // 16, row_unfold)
        for c in range(4):
            far[m, :, c * 256 : (c + 1) * 256] = dot(wide[c], ra_ref[c])

        def terms(step):
            rows = rows16(step)
            parts = [
                (far[m, rows, c * 256 : c * 256 + 128], far[m, rows, c * 256 + 128 : c * 256 + 256])
                for c in range(4)
            ]
            for q, (gr, gi) in enumerate(fold(parts, -1)):
                lanes = slice(q * 128, (q + 1) * 128)
                pr = probe_ref[mode, 0, rows, lanes].astype(F32)
                pi = probe_ref[mode, 1, rows, lanes].astype(F32)
                up_ref[0, rows, lanes] += pr * gr + pi * gi
                up_ref[1, rows, lanes] += pr * gi - pi * gr
                xr, xi = patch[0, rows, lanes], patch[1, rows, lanes]
                out_ref[slot, 0, rows, lanes] = (xr * gr + xi * gi).astype(out_ref.dtype)
                out_ref[slot, 1, rows, lanes] = (xr * gi - xi * gr).astype(out_ref.dtype)

        loop(W // 16, terms)

    loop(2, lambda m: adjoint(m, send_ref, m))
    loop(2, lambda m: adjoint(m + 2, keep_ref, m))

    def clear(step):
        for part, k, lanes in lane_blocks:
            tall[part, k, rows16(step), :] = jnp.zeros((16, 128), F32)
            tall[part, k, rows16(step, W), :] = jnp.zeros((16, 128), F32)

    loop(W // 16, clear)

    def put_rows(step):
        for part, k, lanes in lane_blocks:
            tall[part, k, pl.ds(row_start + step * 16, 16), :] = up_ref[part, rows16(step), lanes]

    loop(W // 16, put_rows)

    def split_rows(step):
        rows = rows16(step)
        for part, k, lanes in lane_blocks:
            up_ref[part, rows, lanes] = tall[part, k, rows, :]
            low_ref[part, rows, lanes] = tall[part, k, rows16(step, W), :].astype(BF16)

    loop(W // 16, split_rows)


def wave(info, own, below, probe, amp):
    tables = [jnp.asarray(t) for t in block_tables()]
    vmem = pl.BlockSpec(memory_space=pltpu.VMEM)
    return pl.pallas_call(
        wave_kernel,
        out_shape=(
            jax.ShapeDtypeStruct((2, W, W), F32),
            jax.ShapeDtypeStruct((2, W, W), BF16),
            jax.ShapeDtypeStruct((2, 2, W, W), BF16),
            jax.ShapeDtypeStruct((2, 2, W, W), F32),
        ),
        in_specs=[pl.BlockSpec(memory_space=pltpu.SMEM)] + [vmem] * 8,
        out_specs=(vmem,) * 4,
        scratch_shapes=[
            pltpu.VMEM((2, 4, 2 * W, 128), F32),
            pltpu.VMEM((2, W, W), F32),
            pltpu.VMEM((4, 256, W), BF16),
            pltpu.VMEM((4, 256, W), F32),
            pltpu.VMEM((4, W, 1024), F32),
            pltpu.VMEM((4, W, 256), BF16),
        ],
        compiler_params=pltpu.CompilerParams(vmem_limit_bytes=52 * MIB),
        cost_estimate=pl.CostEstimate(flops=20 * 10**9, bytes_accessed=20 * MIB, transcendentals=W * W),
        name="wave",
    )(info, own, below, probe, amp, *tables)


def merge_kernel(starts_ref, own_ref, above_ref, out_ref, over_ref, strip):
    lane = lax.broadcasted_iota(jnp.int32, (32, 128), 1)
    zero = jnp.zeros((32, 128), F32)

    def rows_step(step, carry):
        rows = pl.ds(pl.multiple_of(step * 32, 32), 32)
        for part in range(2):
            for k in range(12):
                strip[:, k * 128 : (k + 1) * 128] = zero
            for source, ref in enumerate((own_ref, above_ref)):
                start = starts_ref[source]
                first, shift = start // 128, start % 128
                early = lane < shift
                before = zero
                for k in range(5):
                    if k < 4:
                        value = ref[part, rows, k * 128 : (k + 1) * 128].astype(F32)
                        turned = pltpu.roll(value, shift, 1)
                    else:
                        turned = zero
                    lanes = pl.ds(pl.multiple_of((first + k) * 128, 128), 128)
                    strip[:, lanes] += jnp.where(early, before, turned)
                    before = turned
            out_ref[part, rows, :] = strip[:, :1024]
            over_ref[part, rows, :] = strip[:, 1024:].astype(BF16)
        return carry

    lax.fori_loop(0, own_ref.shape[1] // 32, rows_step, 0)


def merge(starts, own, above):
    vmem = pl.BlockSpec(memory_space=pltpu.VMEM)
    return pl.pallas_call(
        merge_kernel,
        out_shape=(jax.ShapeDtypeStruct((2, W, 1024), F32), jax.ShapeDtypeStruct((2, W, W), BF16)),
        in_specs=[pl.BlockSpec(memory_space=pltpu.SMEM), vmem, vmem],
        out_specs=(vmem, vmem),
        scratch_shapes=[pltpu.VMEM((32, 1536), F32)],
        compiler_params=pltpu.CompilerParams(vmem_limit_bytes=24 * MIB),
        cost_estimate=pl.CostEstimate(flops=8 * MIB, bytes_accessed=8 * MIB, transcendentals=0),
        name="merge",
    )(starts, own, above)


def add_left_kernel(tile_ref, got_ref, out_ref):
    out_ref[...] = tile_ref[...] + got_ref[...].astype(F32)


def add_left(tile, got):
    spec = pl.BlockSpec((2, 128, W), lambda i: (0, i, 0))
    return pl.pallas_call(
        add_left_kernel,
        grid=(4,),
        out_shape=jax.ShapeDtypeStruct(tile.shape, F32),
        in_specs=[spec, spec],
        out_specs=spec,
        input_output_aliases={0: 0},
        compiler_params=pltpu.CompilerParams(vmem_limit_bytes=16 * MIB),
        cost_estimate=pl.CostEstimate(flops=MIB, bytes_accessed=5 * MIB, transcendentals=0),
        name="add_left",
    )(tile, got)


def place_of(index):
    row, col = divmod(index, 16)
    return [col // 2 % 4, row // 2, row % 2 * 2 + col // 8, col % 2]


def index_of(x, y, z, core):
    x, y, z, core = x % 4, y % 4, z % 4, core % 2
    return (y * 2 + z // 2) * 16 + (z % 2 * 4 + x) * 2 + core


def moved(value, axis, distance):
    route = []
    for index in range(128):
        place = place_of(index)
        place[axis] += distance
        route.append((index, index_of(*place)))
    return lax.ppermute(value, AXES, route)


def ring_sum(value, axis, here):
    total = lax.dynamic_index_in_dim(value, here, 0, keepdims=False).astype(F32)
    for distance in (2, 1, 3):
        block = lax.dynamic_index_in_dim(value, (here + distance) % 4, 0, keepdims=False)
        total = total + moved(block.astype(BF16), axis, distance).astype(F32)
    return total


def quarters(value):
    shape = value.shape
    return jnp.moveaxis(value.reshape(shape[0], shape[1], 4, shape[2] // 4, shape[3]), 2, 0)


def probe_sum(send, keep, row, col):
    x, y, z, core = col // 2 % 4, row // 2, row % 2 * 2 + col // 8, col % 2
    total = keep + moved(send, 3, 1).astype(F32)
    total = ring_sum(quarters(total), 1, y)
    total = ring_sum(quarters(total), 2, z)
    total = ring_sum(quarters(total), 0, x)
    mine = lax.dynamic_slice_in_dim(total, core * 4, 4, 2)
    other = moved(lax.dynamic_slice_in_dim(total, (1 - core) * 4, 4, 2), 3, 1)
    even = core == 0
    return jnp.concatenate([jnp.where(even, mine, other), jnp.where(even, other, mine)], axis=0)


def per_device(object_field, probe_modes, positions, amplitudes, live_slots):
    row, col = lax.axis_index("row"), lax.axis_index("col")
    tile_rows, tile_cols = object_field.shape[1:]
    upper = lax.ppermute(positions, "row", [(i, i + 1) for i in range(7)])
    right = lax.ppermute(object_field[:, :, :W], "col", [(i + 1, i) for i in range(15)])
    own_start = positions[0, 1] - col * tile_cols
    upper_start = jnp.clip(upper[0, 1] - col * tile_cols, 0, tile_cols - 1)
    row_start = positions[0, 0] - row * tile_rows
    chosen = window_columns(upper_start[None], object_field, right, "upper_columns")
    below = lax.ppermute(chosen, "row", [(i + 1, i) for i in range(7)])
    own = window_columns(own_start[None], object_field, right, "own_columns")
    amp = amplitude_parts(amplitudes[0])
    info = jnp.stack([row_start, 2 * (1 - col % 2), live_slots[0]]).astype(jnp.int32)
    up, low, send, keep = wave(info, own, below, probe_modes, amp)
    above = lax.ppermute(low, "row", [(i, i + 1) for i in range(7)])
    probe_grad = probe_sum(send, keep, row, col)
    tile, over = merge(jnp.stack([own_start, upper_start]), up, above)
    from_left = lax.ppermute(over, "col", [(i, i + 1) for i in range(15)])
    return add_left(tile, from_left), probe_grad


def solution(mesh):
    placed = (
        P(None, "row", "col"),
        P(),
        P(("row", "col"), None),
        P(("row", "col"), None, None),
        P(("row", "col")),
    )
    return jax.shard_map(
        per_device,
        mesh=mesh,
        in_specs=placed,
        out_specs=(P(None, "row", "col"), P(None, None, ("row", "col"), None)),
        check_vma=False,
    )
```

```python
import functools
import math

import jax
import jax.numpy as jnp
import ml_dtypes
import numpy as np
from jax import lax
from jax.experimental import pallas as pl
from jax.experimental.pallas import tpu as pltpu
from jax.sharding import PartitionSpec as P

W = 512
Q = W // 4
HALF = W // 2
WEIGHT = 100 * 10**9
MIB = 1024 * 1024
F32 = jnp.float32
BF16 = jnp.bfloat16


def block_tables():
    step = np.arange(W).astype(np.float32) * np.float32(2.0 * math.pi / W)
    scale = np.float32(1.0 / math.sqrt(W))
    cos_of = (np.cos(step) * scale).astype(ml_dtypes.bfloat16).astype(np.float32)
    sin_of = (np.sin(step) * scale).astype(ml_dtypes.bfloat16).astype(np.float32)
    short = np.arange(Q)
    forward, adjoint = [], []
    for part in range(4):
        phase = np.outer(4 * short + part, short) % W
        c, s = cos_of[phase], sin_of[phase]
        forward.append(np.block([[c, s], [-s, c]]))
        adjoint.append(np.block([[c.T, -s.T], [s.T, c.T]]))
    forward = np.stack(forward).astype(ml_dtypes.bfloat16)
    adjoint = np.stack(adjoint).astype(ml_dtypes.bfloat16)
    swap = lambda t: np.ascontiguousarray(t.transpose(0, 2, 1))
    return forward, swap(forward), adjoint, swap(adjoint)


def fold(parts, sign):
    (ar, ai), (br, bi), (cr, ci), (dr, di) = parts
    pr, pi, mr, mi = ar + cr, ai + ci, ar - cr, ai - ci
    qr, qi, nr, ni = br + dr, bi + di, br - dr, bi - di
    if sign < 0:
        nr, ni = -nr, -ni
    return (
        (pr + qr, pi + qi),
        (mr + ni, mi - nr),
        (pr - qr, pi - qi),
        (mr - ni, mi + nr),
    )


def dot(a, b):
    return jnp.dot(a, b, preferred_element_type=F32)


def amplitude_kernel(amp_ref, pick_ref, out_ref, sorted_ref):
    rows = amp_ref[...]
    high = rows.astype(BF16)
    rest = rows - high.astype(F32)
    middle = rest.astype(BF16)
    low = (rest - middle.astype(F32)).astype(BF16)
    for c in range(4):
        pick = pick_ref[:, c * Q : (c + 1) * Q]
        sorted_ref[c] = (dot(high, pick) + dot(middle, pick)) + dot(low, pick)
    for c in range(4):
        for r in range(4):
            out_ref[r * Q : (r + 1) * Q, c * Q : (c + 1) * Q] = sorted_ref[c, pl.ds(r, Q, stride=4), :]


def amplitude_parts(amp):
    source = np.arange(W)
    pick = np.zeros((W, W), ml_dtypes.bfloat16)
    pick[source, (source % 4) * Q + source // 4] = 1
    return pl.pallas_call(
        amplitude_kernel,
        out_shape=jax.ShapeDtypeStruct((W, W), F32),
        scratch_shapes=[pltpu.VMEM((4, W, Q), F32)],
        compiler_params=pltpu.CompilerParams(vmem_limit_bytes=16 * MIB),
        cost_estimate=pl.CostEstimate(flops=6 * W**3, bytes_accessed=3 * MIB, transcendentals=0),
        name="amplitude_parts",
    )(amp, jnp.asarray(pick))


def lane_index(block, rows):
    return lax.broadcasted_iota(jnp.int32, (rows, 128), 1) + block * 128


def strip_block(tile_ref, right_ref, part, rows, right_rows, block, start):
    lane = lane_index(block, 16)
    lanes = slice(block * 128, block * 128 + 128)
    first = tile_ref[part, rows, lanes].astype(F32)
    second = tile_ref[part, rows, W + block * 128 : W + block * 128 + 128].astype(F32)
    beyond = right_ref[part, right_rows, lanes].astype(F32)
    return jnp.where(lane >= start, first, jnp.where(lane >= start - W, second, beyond))


def row_steps(count, size, body):
    def step_of(step, carry):
        body(pl.ds(pl.multiple_of(step * size, size), size))
        return carry

    lax.fori_loop(0, count // size, step_of, 0)


def columns_kernel(start_ref, tile_ref, right_ref, out_ref):
    def body(rows):
        for part in range(2):
            for block in range(4):
                value = strip_block(tile_ref, right_ref, part, rows, rows, block, start_ref[0])
                out_ref[part, rows, block * 128 : block * 128 + 128] = value.astype(BF16)

    row_steps(out_ref.shape[1], 16, body)


def window_columns(start, tile, right, chunk):
    rows = right.shape[1]
    whole = pl.BlockSpec((2, rows, W), lambda i: (0, 0, 0))
    return pl.pallas_call(
        columns_kernel,
        grid=(1,),
        out_shape=jax.ShapeDtypeStruct((2, rows, W), BF16),
        in_specs=[
            pl.BlockSpec(memory_space=pltpu.SMEM),
            pl.BlockSpec((2, rows, 1024), lambda i: (0, chunk, 0)),
            whole,
        ],
        out_specs=whole,
        compiler_params=pltpu.CompilerParams(vmem_limit_bytes=16 * MIB),
        cost_estimate=pl.CostEstimate(flops=WEIGHT, bytes_accessed=2 * MIB, transcendentals=0),
        name="window_columns",
    )(start, tile, right)


def copy_kernel(tile_ref, out_ref):
    out_ref[...] = tile_ref[...]


def left_columns(tile, chunk, rows):
    return pl.pallas_call(
        copy_kernel,
        grid=(1,),
        out_shape=jax.ShapeDtypeStruct((2, rows, W), BF16),
        in_specs=[pl.BlockSpec((2, rows, W), lambda i: (0, chunk, 0))],
        out_specs=pl.BlockSpec((2, rows, W), lambda i: (0, 0, 0)),
        compiler_params=pltpu.CompilerParams(vmem_limit_bytes=16 * MIB),
        cost_estimate=pl.CostEstimate(flops=0, bytes_accessed=MIB, transcendentals=0),
        name="left_columns",
    )(tile)


def wave_kernel(
    info_ref, own0_ref, own1_ref, below0_ref, below1_ref, probe_hbm, amp_hbm, lf_ref, rf_ref, la_ref, ra_ref,
    up_ref, low_ref, send_hbm, keep_hbm,
    tall, patch, folded0, folded1, mid0, mid1, wide0, wide1, far, waves, probe, amp, terms_out,
    probe_sem, amp_sem, out_sem,
):
    row_start = info_ref[0]
    first_mode = info_ref[1]
    live = info_ref[2].astype(F32)
    col_start = info_ref[3]
    turn_block, turn = col_start % W // 128, col_start % 128
    folded, mid, wide = (folded0, folded1), (mid0, mid1), (wide0, wide1)

    def loop(count, body, unroll=1):
        lax.fori_loop(0, count, lambda i, c: (body(i), c)[1], 0, unroll=unroll)

    def rows16(step, base=0):
        if isinstance(step, int):
            return slice(base + step * 16, base + step * 16 + 16)
        return pl.ds(pl.multiple_of(base + step * 16, 16), 16)

    def probe_copy(m):
        mode = lax.rem(m + first_mode, 4)
        return pltpu.make_async_copy(probe_hbm.at[mode], probe.at[m], probe_sem.at[m])

    def terms_copy(m):
        target = send_hbm.at[m] if m < 2 else keep_hbm.at[m - 2]
        return pltpu.make_async_copy(terms_out.at[m], target, out_sem.at[m])

    amp_copy = pltpu.make_async_copy(amp_hbm, amp, amp_sem)
    for m in range(4):
        probe_copy(m).start()
    amp_copy.start()

    blocks = [slice(k * 128, (k + 1) * 128) for k in range(4)]
    lane_blocks = [(part, k, blocks[k]) for part in range(2) for k in range(4)]

    def stack_rows(step):
        for part, k, lanes in lane_blocks:
            for h, ref in enumerate((own0_ref, own1_ref, below0_ref, below1_ref)):
                tall[part, k, rows16(step, h * HALF), :] = ref[part, rows16(step), lanes].astype(F32)

    loop(HALF // 16, stack_rows, 2)
    lane16 = lax.broadcasted_iota(jnp.int32, (16, 128), 1)

    def take_rows(step):
        for part in range(2):
            turned = []
            for k in range(4):
                value = tall[part, (turn_block + k) % 4, pl.ds(row_start + step * 16, 16), :]
                turned.append(pltpu.roll(value, (128 - turn) % 128, 1))
            for k, lanes in enumerate(blocks):
                value = jnp.where(lane16 < 128 - turn, turned[k], turned[(k + 1) % 4])
                patch[part, rows16(step), lanes] = value

    loop(W // 16, take_rows, 4)

    def exit_fold(m, quarter):
        for step in (quarter * 2, quarter * 2 + 1):
            for lanes in blocks:
                parts = []
                for q in range(4):
                    rows = rows16(step, q * Q)
                    pr = probe[m, 0, rows, lanes].astype(F32)
                    pi = probe[m, 1, rows, lanes].astype(F32)
                    xr, xi = patch[0, rows, lanes], patch[1, rows, lanes]
                    er = (pr * xr - pi * xi).astype(BF16).astype(F32)
                    ei = (pr * xi + pi * xr).astype(BF16).astype(F32)
                    parts.append((er, ei))
                for r, (zr, zi) in enumerate(fold(parts, 1)):
                    folded[m % 2][r, rows16(step), lanes] = zr.astype(BF16)
                    folded[m % 2][r, rows16(step, Q), lanes] = zi.astype(BF16)

    def column_fold(m, r):
        for step in range(Q // 16):
            parts = []
            for lanes in blocks:
                yr = mid[m % 2][r, rows16(step), lanes].astype(BF16).astype(F32)
                yi = mid[m % 2][r, rows16(step, Q), lanes].astype(BF16).astype(F32)
                parts.append((yr, yi))
            for c, (wr, wi) in enumerate(fold(parts, 1)):
                wide[m % 2][c, rows16(step, r * Q), 0:128] = wr.astype(BF16)
                wide[m % 2][c, rows16(step, r * Q), 128:256] = wi.astype(BF16)

    def forward_step(tick, i):
        if tick < 4:
            exit_fold(tick, i)
        if 0 <= tick - 1 < 4:
            mid[(tick - 1) % 2][i] = dot(lf_ref[i], folded[(tick - 1) % 2][i])
        if 0 <= tick - 2 < 4:
            column_fold(tick - 2, i)
        if 0 <= tick - 3 < 4:
            far[tick - 3, i] = dot(wide[(tick - 3) % 2][i], rf_ref[i])

    for tick in range(7):
        if tick < 4:
            probe_copy(tick).wait()
        [forward_step(tick, i) for i in range(4)]

    amp_copy.wait()

    def residual(step):
        r, inner = step // 8, step % 8
        rows = rows16(step)
        for c, lanes in enumerate(blocks):
            fields = [(far[m, c, rows, 0:128], far[m, c, rows, 128:256]) for m in range(4)]
            intensity = sum(fr * fr + fi * fi for fr, fi in fields)
            ratio = live * (1.0 - amp[rows, lanes] * lax.rsqrt(jnp.maximum(intensity, 0.25)))
            for m, (fr, fi) in enumerate(fields):
                waves[m, r, rows16(inner), lanes] = (fr * ratio).astype(BF16)
                waves[m, r, rows16(inner, Q), lanes] = (fi * ratio).astype(BF16)

    loop(W // 16, residual, 2)

    def row_unfold(m, c):
        lanes = blocks[c]
        for step in range(Q // 16):
            parts = [
                (mid[m % 2][r, rows16(step), lanes], mid[m % 2][r, rows16(step, Q), lanes])
                for r in range(4)
            ]
            for q, (yr, yi) in enumerate(fold(parts, -1)):
                wide[m % 2][c, rows16(step, q * Q), 0:128] = yr.astype(BF16)
                wide[m % 2][c, rows16(step, q * Q), 128:256] = yi.astype(BF16)

    def terms(m, quarter):
        for step in range(8):
            rows = rows16(quarter * 8 + step)
            parts = [(far[m, c, rows, 0:128], far[m, c, rows, 128:256]) for c in range(4)]
            for lanes, (gr, gi) in zip(blocks, fold(parts, -1)):
                pr = probe[m, 0, rows, lanes].astype(F32)
                pi = probe[m, 1, rows, lanes].astype(F32)
                object_r, object_i = pr * gr + pi * gi, pr * gi - pi * gr
                if m:
                    object_r = object_r + up_ref[0, rows, lanes]
                    object_i = object_i + up_ref[1, rows, lanes]
                up_ref[0, rows, lanes] = object_r
                up_ref[1, rows, lanes] = object_i
                xr, xi = patch[0, rows, lanes], patch[1, rows, lanes]
                terms_out[m, 0, rows, lanes] = (xr * gr + xi * gi).astype(BF16)
                terms_out[m, 1, rows, lanes] = (xr * gi - xi * gr).astype(BF16)

    def adjoint_step(tick, i):
        if tick < 4:
            mid[tick % 2][i] = dot(la_ref[i], waves[tick, i])
        if 0 <= tick - 1 < 4:
            row_unfold(tick - 1, i)
        if 0 <= tick - 2 < 4:
            far[tick - 2, i] = dot(wide[(tick - 2) % 2][i], ra_ref[i])
        if 0 <= tick - 3 < 4:
            terms(tick - 3, i)

    for tick in range(7):
        [adjoint_step(tick, i) for i in range(4)]
        if tick >= 3:
            terms_copy(tick - 3).start()

    def clear(step):
        for part, k, lanes in lane_blocks:
            tall[part, k, rows16(step), :] = jnp.zeros((16, 128), F32)
            tall[part, k, rows16(step, W), :] = jnp.zeros((16, 128), F32)

    loop(W // 16, clear, 2)

    def put_rows(step):
        for part in range(2):
            turned = [pltpu.roll(up_ref[part, rows16(step), lanes], turn, 1) for lanes in blocks]
            for k in range(4):
                value = jnp.where(lane16 < turn, turned[(k + 3) % 4], turned[k])
                tall[part, (turn_block + k) % 4, pl.ds(row_start + step * 16, 16), :] = value

    loop(W // 16, put_rows, 4)

    def split_rows(step):
        rows = rows16(step)
        for part, k, lanes in lane_blocks:
            up_ref[part, rows, lanes] = tall[part, k, rows, :]
            low_ref[part, rows, lanes] = tall[part, k, rows16(step, W), :].astype(BF16)

    loop(W // 16, split_rows, 2)
    for m in range(4):
        terms_copy(m).wait()


def wave(info, own0, own1, below0, below1, probe, amp):
    tables = [jnp.asarray(t) for t in block_tables()]
    vmem = pl.BlockSpec(memory_space=pltpu.VMEM)
    hbm = pl.BlockSpec(memory_space=pl.ANY)
    return pl.pallas_call(
        wave_kernel,
        out_shape=(
            jax.ShapeDtypeStruct((2, W, W), F32),
            jax.ShapeDtypeStruct((2, W, W), BF16),
            jax.ShapeDtypeStruct((2, 2, W, W), BF16),
            jax.ShapeDtypeStruct((2, 2, W, W), BF16),
        ),
        in_specs=[pl.BlockSpec(memory_space=pltpu.SMEM), vmem, vmem, vmem, vmem, hbm, hbm] + [vmem] * 4,
        out_specs=(vmem, vmem, hbm, hbm),
        scratch_shapes=[
            pltpu.VMEM((2, 4, 2 * W, 128), F32),
            pltpu.VMEM((2, W, W), F32),
            pltpu.VMEM((4, 256, W), BF16),
            pltpu.VMEM((4, 256, W), BF16),
            pltpu.VMEM((4, 256, W), F32),
            pltpu.VMEM((4, 256, W), F32),
            pltpu.VMEM((4, W, 256), BF16),
            pltpu.VMEM((4, W, 256), BF16),
            pltpu.VMEM((4, 4, W, 256), F32),
            pltpu.VMEM((4, 4, 256, W), BF16),
            pltpu.VMEM((4, 2, W, W), BF16),
            pltpu.VMEM((W, W), F32),
            pltpu.VMEM((4, 2, W, W), BF16),
            pltpu.SemaphoreType.DMA((4,)),
            pltpu.SemaphoreType.DMA,
            pltpu.SemaphoreType.DMA((4,)),
        ],
        compiler_params=pltpu.CompilerParams(vmem_limit_bytes=54 * MIB),
        cost_estimate=pl.CostEstimate(flops=20 * 10**9, bytes_accessed=20 * MIB, transcendentals=W * W),
        name="wave",
    )(info, own0, own1, below0, below1, probe, amp, *tables)


def over_kernel(starts_ref, up_ref, above_ref, after_ref, out_ref):
    def body(rows):
        for part in range(2):
            for block in range(4):
                lanes = slice(block * 128, block * 128 + 128)
                total = jnp.zeros((16, 128), F32)
                for source, ref in enumerate((up_ref, above_ref)):
                    passes = lane_index(block, 16) < starts_ref[source] - W
                    total = total + jnp.where(passes, ref[part, rows, lanes].astype(F32), 0.0)
                out_ref[part, rows, lanes] = total.astype(BF16)

    row_steps(out_ref.shape[1], 16, body)


def overflow(starts, up, above, after):
    whole = pl.BlockSpec((2, 128, W), lambda i: (0, i, 0))
    return pl.pallas_call(
        over_kernel,
        grid=(4,),
        out_shape=jax.ShapeDtypeStruct((2, W, W), BF16),
        in_specs=[
            pl.BlockSpec(memory_space=pltpu.SMEM),
            whole,
            whole,
            pl.BlockSpec(memory_space=pl.ANY),
        ],
        out_specs=whole,
        compiler_params=pltpu.CompilerParams(vmem_limit_bytes=16 * MIB),
        cost_estimate=pl.CostEstimate(flops=WEIGHT, bytes_accessed=2 * MIB, transcendentals=0),
        name="overflow",
    )(starts, up, above, after)


def finish_kernel(starts_ref, up_ref, above_ref, left_ref, after_ref, out_ref):
    masks = []
    for block in range(4):
        lane = lane_index(block, 16)
        for source in range(2):
            start = starts_ref[source]
            masks.append((lane >= start, jnp.logical_and(lane < start, lane >= start - W)))

    def body(rows):
        for part in range(2):
            for block in range(4):
                lanes = slice(block * 128, block * 128 + 128)
                low = left_ref[part, rows, lanes].astype(F32)
                high = jnp.zeros((16, 128), F32)
                for source, ref in enumerate((up_ref, above_ref)):
                    in_first, in_second = masks[block * 2 + source]
                    value = ref[part, rows, lanes].astype(F32)
                    low = low + jnp.where(in_first, value, 0.0)
                    high = high + jnp.where(in_second, value, 0.0)
                out_ref[part, rows, lanes] = low
                out_ref[part, rows, W + block * 128 : W + block * 128 + 128] = high

    row_steps(out_ref.shape[1], 16, body)


def finish(starts, up, above, left, after):
    size = 64
    spec = lambda columns: pl.BlockSpec((2, size, columns), lambda i: (0, i, 0))
    return pl.pallas_call(
        finish_kernel,
        grid=(W // size,),
        out_shape=jax.ShapeDtypeStruct((2, W, 1024), F32),
        in_specs=[pl.BlockSpec(memory_space=pltpu.SMEM)] + [spec(W)] * 3 + [pl.BlockSpec(memory_space=pl.ANY)],
        out_specs=spec(1024),
        compiler_params=pltpu.CompilerParams(vmem_limit_bytes=16 * MIB),
        cost_estimate=pl.CostEstimate(flops=4 * MIB, bytes_accessed=8 * MIB, transcendentals=0),
        name="finish",
    )(starts, up, above, left, after)


def chip_sum_kernel(keep_ref, got_ref, out_ref):
    def body(rows):
        for mode in range(2):
            for part in range(2):
                total = keep_ref[mode, part, rows, :].astype(F32) + got_ref[mode, part, rows, :].astype(F32)
                short = pl.ds(pl.multiple_of(rows.start // 4, 16), 16)
                for x in range(4):
                    group = [total[x * 8 : x * 8 + 8], total[32 + x * 8 : 40 + x * 8]]
                    out_ref[x, mode, part, short, :] = jnp.concatenate(group, axis=0).astype(BF16)

    row_steps(Q, 64, body)


def chip_sum(keep, got):
    spec = pl.BlockSpec((2, 2, Q, W), lambda i: (0, 0, i, 0))
    return pl.pallas_call(
        chip_sum_kernel,
        grid=(4,),
        out_shape=jax.ShapeDtypeStruct((4, 2, 2, Q, W), BF16),
        in_specs=[spec, spec],
        out_specs=pl.BlockSpec((4, 2, 2, Q // 4, W), lambda i: (0, 0, 0, i, 0)),
        compiler_params=pltpu.CompilerParams(vmem_limit_bytes=16 * MIB),
        cost_estimate=pl.CostEstimate(flops=WEIGHT, bytes_accessed=6 * MIB, transcendentals=0),
        name="chip_sum",
    )(keep, got)


ROW = ("y", "z_hi")
COL = ("z_lo", "x", "core")


def chips_sum(send, keep):
    got = lax.ppermute(send, "core", [(0, 1), (1, 0)])
    blocks = chip_sum(keep, got)
    return blocks, lax.all_to_all(blocks, "x", 0, 0, tiled=True)


def row_blocks_kernel(got_ref, out_ref):
    upper = lax.broadcasted_iota(jnp.int32, (8, W), 0) < 4

    def body(rows):
        totals = []
        for mode in range(2):
            for part in range(2):
                totals.append(sum(got_ref[k, mode, part, rows, :].astype(F32) for k in range(4)))
        for half in range(2):
            pieces = [total[half * 8 : half * 8 + 8] for total in totals]
            turned = [pltpu.roll(piece, 4, 0) for piece in pieces]
            for core in range(2):
                pair = []
                for k in (0, 2):
                    if core == 0:
                        pair.append(jnp.where(upper, pieces[k], turned[k + 1]))
                    else:
                        pair.append(jnp.where(upper, turned[k], pieces[k + 1]))
                place = rows.start // 4 + half * 2 + core
                out_ref[place] = jnp.concatenate(pair, axis=0).astype(BF16)

    row_steps(got_ref.shape[3], 16, body)


def row_blocks(got):
    return pl.pallas_call(
        row_blocks_kernel,
        grid=(4,),
        out_shape=jax.ShapeDtypeStruct((32, 16, W), BF16),
        in_specs=[pl.BlockSpec((4, 2, 2, Q // 4, W), lambda i: (0, 0, 0, i, 0))],
        out_specs=pl.BlockSpec((8, 16, W), lambda i: (i, 0, 0)),
        compiler_params=pltpu.CompilerParams(vmem_limit_bytes=16 * MIB),
        cost_estimate=pl.CostEstimate(flops=MIB, bytes_accessed=3 * MIB, transcendentals=0),
        name="row_blocks",
    )(got)


def rows_sum(blocks):
    got = lax.all_to_all(blocks, ("y", "z_hi", "z_lo", "core"), 0, 0, tiled=True)
    return got.astype(F32).reshape(16, 2, 16, W).sum(0).reshape(4, 2, 4, W)


def per_device(object_field, probe_modes, positions, amplitudes, live_slots):
    row, col = lax.axis_index(ROW), lax.axis_index(COL)
    tile_rows, tile_cols = object_field.shape[1:]
    to_left = [(i + 1, i) for i in range(15)]
    to_right = [(i, i + 1) for i in range(15)]
    to_upper = [(i + 1, i) for i in range(7)]
    to_lower = [(i, i + 1) for i in range(7)]
    upper = lax.ppermute(positions, ROW, to_lower)
    right = [lax.ppermute(left_columns(object_field, h, HALF), COL, to_left) for h in range(2)]
    own_start = positions[:, 1] - col * tile_cols
    upper_start = jnp.clip(upper[:, 1] - col * tile_cols, 0, tile_cols - 1)
    row_start = positions[0, 0] - row * tile_rows
    chosen = [window_columns(upper_start, object_field, right[h], h) for h in range(2)]
    below = [lax.ppermute(chosen[h], ROW, to_upper) for h in range(2)]
    own = [window_columns(own_start, object_field, right[h], h) for h in range(2)]
    amp = amplitude_parts(amplitudes[0])
    first_mode = 2 * (1 - lax.axis_index("core"))
    info = jnp.stack([row_start, first_mode, live_slots[0], own_start[0]]).astype(jnp.int32)
    up, low, send, keep = wave(info, *own, *below, probe_modes, amp)
    above = lax.ppermute(low, ROW, to_lower)
    chip_terms, chips_terms = chips_sum(send, keep)
    starts = jnp.concatenate([own_start, upper_start])
    left = lax.ppermute(overflow(starts, up, above, chip_terms), COL, to_right)
    row_terms = row_blocks(chips_terms)
    probe_grad = rows_sum(row_terms)
    return finish(starts, up, above, left, row_terms), probe_grad


def solution(mesh):
    chips = jax.sharding.Mesh(mesh.devices.reshape(4, 2, 2, 4, 2), ROW + COL)
    slots = ROW + COL
    placed = (P(None, ROW, COL), P(), P(slots, None), P(slots, None, None), P(slots))
    return jax.shard_map(
        per_device,
        mesh=chips,
        in_specs=placed,
        out_specs=(P(None, ROW, COL), P(None, None, slots, None)),
        check_vma=False,
    )
```

```python
import functools
import math

import jax
import jax.numpy as jnp
import ml_dtypes
import numpy as np
from jax import lax
from jax.experimental import pallas as pl
from jax.experimental.pallas import tpu as pltpu
from jax.sharding import PartitionSpec as P

W = 512
Q = W // 4
HALF = W // 2
WEIGHT = 100 * 10**9
MIB = 1024 * 1024
F32 = jnp.float32
BF16 = jnp.bfloat16


def block_tables():
    step = np.arange(W).astype(np.float32) * np.float32(2.0 * math.pi / W)
    scale = np.float32(1.0 / math.sqrt(W))
    cos_of = (np.cos(step) * scale).astype(ml_dtypes.bfloat16).astype(np.float32)
    sin_of = (np.sin(step) * scale).astype(ml_dtypes.bfloat16).astype(np.float32)
    short = np.arange(Q)
    forward = []
    for part in range(4):
        phase = np.outer(4 * short + part, short) % W
        c, s = cos_of[phase], sin_of[phase]
        forward.append(np.block([[c, s], [-s, c]]))
    forward = np.stack(forward).astype(ml_dtypes.bfloat16)
    return forward, np.ascontiguousarray(forward.transpose(0, 2, 1))


def fold(parts, sign):
    (ar, ai), (br, bi), (cr, ci), (dr, di) = parts
    pr, pi, mr, mi = ar + cr, ai + ci, ar - cr, ai - ci
    qr, qi, nr, ni = br + dr, bi + di, br - dr, bi - di
    if sign < 0:
        nr, ni = -nr, -ni
    return (
        (pr + qr, pi + qi),
        (mr + ni, mi - nr),
        (pr - qr, pi - qi),
        (mr - ni, mi + nr),
    )


def dot(a, b):
    return jnp.dot(a, b, preferred_element_type=F32)


def amplitude_kernel(amp_ref, pick_ref, after_ref, out_ref, sorted_ref):
    rows = amp_ref[...]
    high = rows.astype(BF16)
    rest = rows - high.astype(F32)
    middle = rest.astype(BF16)
    low = (rest - middle.astype(F32)).astype(BF16)
    for c in range(4):
        pick = pick_ref[:, c * Q : (c + 1) * Q]
        sorted_ref[c] = (dot(high, pick) + dot(middle, pick)) + dot(low, pick)
    for c in range(4):
        for r in range(4):
            out_ref[r * Q : (r + 1) * Q, c * Q : (c + 1) * Q] = sorted_ref[c, pl.ds(r, Q, stride=4), :]


def amplitude_parts(amp, after):
    source = np.arange(W)
    pick = np.zeros((W, W), ml_dtypes.bfloat16)
    pick[source, (source % 4) * Q + source // 4] = 1
    return pl.pallas_call(
        amplitude_kernel,
        out_shape=jax.ShapeDtypeStruct((W, W), F32),
        in_specs=[pl.BlockSpec(memory_space=pltpu.VMEM)] * 2 + [pl.BlockSpec(memory_space=pl.ANY)],
        scratch_shapes=[pltpu.VMEM((4, W, Q), F32)],
        compiler_params=pltpu.CompilerParams(vmem_limit_bytes=16 * MIB),
        cost_estimate=pl.CostEstimate(flops=6 * W**3, bytes_accessed=3 * MIB, transcendentals=0),
        name="amplitude_parts",
    )(amp, jnp.asarray(pick), after)


def overflow(own_start, up, upper_start, above):
    lane = lax.broadcasted_iota(jnp.int32, up.shape, 2)
    own = jnp.where(lane < own_start - W, up.astype(F32), 0.0)
    return (own + jnp.where(lane < upper_start - W, above.astype(F32), 0.0)).astype(BF16)


def lane_index(block, rows):
    return lax.broadcasted_iota(jnp.int32, (rows, 128), 1) + block * 128


def row_steps(count, size, body, unroll=1):
    def step_of(step, carry):
        body(pl.ds(pl.multiple_of(step * size, size), size))
        return carry

    lax.fori_loop(0, count // size, step_of, 0, unroll=unroll)


def columns_kernel(corner_ref, anchor_ref, tile_ref, right_ref, out_ref):
    start = jnp.clip(corner_ref[0, 1] - anchor_ref[0], 0, 2 * W - 1)
    masks = [(lane_index(k, 16) >= start, lane_index(k, 16) >= start - W) for k in range(4)]

    def body(rows):
        for part in range(2):
            for k, (in_first, in_second) in enumerate(masks):
                lanes = slice(k * 128, k * 128 + 128)
                first = tile_ref[part, rows, lanes].astype(F32)
                second = tile_ref[part, rows, W + k * 128 : W + k * 128 + 128].astype(F32)
                beyond = right_ref[part, rows, lanes].astype(F32)
                value = jnp.where(in_first, first, jnp.where(in_second, second, beyond))
                out_ref[part, rows, lanes] = value.astype(BF16)

    row_steps(out_ref.shape[1], 16, body, 2)


def cut_columns(corner, anchor, tile, right, chunk):
    rows = right.shape[1]
    whole = pl.BlockSpec((2, rows, W), lambda i: (0, 0, 0))
    return pl.pallas_call(
        columns_kernel,
        grid=(1,),
        out_shape=jax.ShapeDtypeStruct((2, rows, W), BF16),
        in_specs=[
            pl.BlockSpec(memory_space=pltpu.SMEM),
            pl.BlockSpec(memory_space=pltpu.SMEM),
            pl.BlockSpec((2, rows, 2 * W), lambda i: (0, chunk, 0)),
            whole,
        ],
        out_specs=whole,
        compiler_params=pltpu.CompilerParams(vmem_limit_bytes=16 * MIB),
        cost_estimate=pl.CostEstimate(flops=WEIGHT, bytes_accessed=2 * MIB, transcendentals=0),
        name="cut_columns",
    )(corner, anchor, tile, right)


def copy_kernel(tile_ref, out_ref):
    out_ref[...] = tile_ref[...]


def left_columns(tile, chunk, rows):
    return pl.pallas_call(
        copy_kernel,
        grid=(1,),
        out_shape=jax.ShapeDtypeStruct((2, rows, W), BF16),
        in_specs=[pl.BlockSpec((2, rows, W), lambda i: (0, chunk, 0))],
        out_specs=pl.BlockSpec((2, rows, W), lambda i: (0, 0, 0)),
        compiler_params=pltpu.CompilerParams(vmem_limit_bytes=16 * MIB),
        cost_estimate=pl.CostEstimate(flops=0, bytes_accessed=MIB, transcendentals=0),
        name="left_columns",
    )(tile)


def wave_kernel(
    info_ref, own0_ref, own1_ref, below0_ref, below1_ref, probe_hbm, amp_hbm, forward_ref, adjoint_ref,
    up_ref, low_ref, send_hbm, keep_hbm,
    tall, patch, folded0, folded1, mid0, mid1, wide0, wide1, far, waves, probe, amp, terms_out, object_sum,
    probe_sem, amp_sem, out_sem,
):
    row_start = info_ref[0]
    core = info_ref[1]
    live = info_ref[2].astype(F32)
    col_start = info_ref[3]
    turn_block, turn = col_start % W // 128, col_start % 128
    folded, mid, wide = (folded0, folded1), (mid0, mid1), (wide0, wide1)

    def loop(count, body, unroll=1):
        lax.fori_loop(0, count, lambda i, c: (body(i), c)[1], 0, unroll=unroll)

    def rows16(step, base=0):
        if isinstance(step, int):
            return slice(base + step * 16, base + step * 16 + 16)
        return pl.ds(pl.multiple_of(base + step * 16, 16), 16)

    def probe_copy(m):
        return pltpu.make_async_copy(probe_hbm.at[m], probe.at[m], probe_sem.at[m])

    def send_copy(m):
        return pltpu.make_async_copy(terms_out.at[m, 1 - core], send_hbm.at[m], out_sem.at[m])

    def keep_copy(m):
        return pltpu.make_async_copy(terms_out.at[m, core], keep_hbm.at[m], out_sem.at[4 + m])

    amp_copy = pltpu.make_async_copy(amp_hbm, amp, amp_sem)
    for m in range(4):
        probe_copy(m).start()
    amp_copy.start()

    blocks = [slice(k * 128, (k + 1) * 128) for k in range(4)]
    lane_blocks = [(part, k, blocks[k]) for part in range(2) for k in range(4)]

    def stack_rows(step):
        for part, k, lanes in lane_blocks:
            for h, ref in enumerate((own0_ref, own1_ref, below0_ref, below1_ref)):
                tall[part, k, rows16(step, h * HALF), :] = ref[part, rows16(step), lanes].astype(F32)

    loop(HALF // 16, stack_rows, 2)
    lane16 = lax.broadcasted_iota(jnp.int32, (16, 128), 1)

    def take_rows(step):
        for part in range(2):
            turned = []
            for k in range(4):
                value = tall[part, (turn_block + k) % 4, pl.ds(row_start + step * 16, 16), :]
                turned.append(pltpu.roll(value, (128 - turn) % 128, 1))
            for k, lanes in enumerate(blocks):
                value = jnp.where(lane16 < 128 - turn, turned[k], turned[(k + 1) % 4])
                patch[part, rows16(step), lanes] = value

    loop(W // 16, take_rows, 4)

    def exit_fold(m, quarter):
        for step in (quarter * 2, quarter * 2 + 1):
            for lanes in blocks:
                parts = []
                for q in range(4):
                    rows = rows16(step, q * Q)
                    pr = probe[m, 0, rows, lanes].astype(F32)
                    pi = probe[m, 1, rows, lanes].astype(F32)
                    xr, xi = patch[0, rows, lanes], patch[1, rows, lanes]
                    er = (pr * xr - pi * xi).astype(BF16).astype(F32)
                    ei = (pr * xi + pi * xr).astype(BF16).astype(F32)
                    parts.append((er, ei))
                for r, (zr, zi) in enumerate(fold(parts, 1)):
                    folded[m % 2][r, rows16(step), lanes] = zr.astype(BF16)
                    folded[m % 2][r, rows16(step, Q), lanes] = zi.astype(BF16)

    def column_fold(m, r):
        for step in range(Q // 16):
            parts = []
            for lanes in blocks:
                yr = mid[m % 2][r, rows16(step), lanes].astype(BF16).astype(F32)
                yi = mid[m % 2][r, rows16(step, Q), lanes].astype(BF16).astype(F32)
                parts.append((yr, yi))
            for c, (wr, wi) in enumerate(fold(parts, 1)):
                wide[m % 2][c, rows16(step, r * Q), 0:128] = wr.astype(BF16)
                wide[m % 2][c, rows16(step, r * Q), 128:256] = wi.astype(BF16)

    def forward_step(tick, i):
        if tick < 4:
            exit_fold(tick, i)
        if 0 <= tick - 1 < 4:
            mid[(tick - 1) % 2][i] = dot(forward_ref[i], folded[(tick - 1) % 2][i])
        if 0 <= tick - 2 < 4:
            column_fold(tick - 2, i)
        if 0 <= tick - 3 < 4:
            far[tick - 3, i] = dot(wide[(tick - 3) % 2][i], adjoint_ref[i])

    for tick in range(7):
        if tick < 4:
            probe_copy(tick).wait()
        [forward_step(tick, i) for i in range(4)]

    amp_copy.wait()

    def residual(step):
        r, inner = step // 8, step % 8
        rows = rows16(step)
        for c, lanes in enumerate(blocks):
            fields = [(far[m, c, rows, 0:128], far[m, c, rows, 128:256]) for m in range(4)]
            intensity = sum(fr * fr + fi * fi for fr, fi in fields)
            ratio = live * (1.0 - amp[rows, lanes] * lax.rsqrt(jnp.maximum(intensity, 0.25)))
            for m, (fr, fi) in enumerate(fields):
                waves[m, r, rows16(inner), lanes] = (fr * ratio).astype(BF16)
                waves[m, r, rows16(inner, Q), lanes] = (fi * ratio).astype(BF16)

    loop(W // 16, residual, 2)

    def row_unfold(m, c):
        lanes = blocks[c]
        for step in range(Q // 16):
            parts = [
                (mid[m % 2][r, rows16(step), lanes], mid[m % 2][r, rows16(step, Q), lanes])
                for r in range(4)
            ]
            for q, (yr, yi) in enumerate(fold(parts, -1)):
                wide[m % 2][c, rows16(step, q * Q), 0:128] = yr.astype(BF16)
                wide[m % 2][c, rows16(step, q * Q), 128:256] = yi.astype(BF16)

    upper8 = lax.broadcasted_iota(jnp.int32, (8, 128), 0) < 4

    def by_core(value):
        pieces = [value[k * 8 : k * 8 + 8] for k in range(4)]
        turned = [pltpu.roll(piece, 4, 0) for piece in pieces]
        first = [jnp.where(upper8, pieces[k], turned[k + 1]) for k in (0, 2)]
        second = [jnp.where(upper8, turned[k], pieces[k + 1]) for k in (0, 2)]
        return [jnp.concatenate(half, axis=0).astype(BF16) for half in (first, second)]

    def terms(m, quarter):
        for step in range(4):
            start = quarter * 128 + step * 32
            rows, short = slice(start, start + 32), slice(start // 2, start // 2 + 16)
            parts = [(far[m, c, rows, 0:128], far[m, c, rows, 128:256]) for c in range(4)]
            for lanes, (gr, gi) in zip(blocks, fold(parts, -1)):
                pr = probe[m, 0, rows, lanes].astype(F32)
                pi = probe[m, 1, rows, lanes].astype(F32)
                object_r, object_i = pr * gr + pi * gi, pr * gi - pi * gr
                if m:
                    object_r = object_r + object_sum[0, rows, lanes]
                    object_i = object_i + object_sum[1, rows, lanes]
                object_sum[0, rows, lanes] = object_r
                object_sum[1, rows, lanes] = object_i
                xr, xi = patch[0, rows, lanes], patch[1, rows, lanes]
                for part, term in enumerate((xr * gr + xi * gi, xr * gi - xi * gr)):
                    for half, value in enumerate(by_core(term)):
                        terms_out[m, half, part, short, lanes] = value

    def adjoint_step(tick, i):
        if tick < 4:
            mid[tick % 2][i] = dot(adjoint_ref[i], waves[tick, i])
        if 0 <= tick - 1 < 4:
            row_unfold(tick - 1, i)
        if 0 <= tick - 2 < 4:
            far[tick - 2, i] = dot(wide[(tick - 2) % 2][i], forward_ref[i])
        if 0 <= tick - 3 < 4:
            terms(tick - 3, i)

    for tick in range(7):
        [adjoint_step(tick, i) for i in range(4)]
        if tick >= 3:
            send_copy(tick - 3).start()
            keep_copy(tick - 3).start()

    def clear(step):
        for part, k, lanes in lane_blocks:
            tall[part, k, rows16(step), :] = jnp.zeros((16, 128), F32)
            tall[part, k, rows16(step, W), :] = jnp.zeros((16, 128), F32)

    loop(W // 16, clear, 2)

    def put_rows(step):
        for part in range(2):
            turned = [pltpu.roll(object_sum[part, rows16(step), lanes], turn, 1) for lanes in blocks]
            for k in range(4):
                value = jnp.where(lane16 < turn, turned[(k + 3) % 4], turned[k])
                tall[part, (turn_block + k) % 4, pl.ds(row_start + step * 16, 16), :] = value

    loop(W // 16, put_rows, 4)

    def split_rows(step):
        rows = rows16(step)
        for part, k, lanes in lane_blocks:
            up_ref[part, rows, lanes] = tall[part, k, rows, :].astype(BF16)
            low_ref[part, rows, lanes] = tall[part, k, rows16(step, W), :].astype(BF16)

    loop(W // 16, split_rows, 2)
    for m in range(4):
        send_copy(m).wait()
        keep_copy(m).wait()


def wave(info, own0, own1, below0, below1, probe, amp):
    tables = [jnp.asarray(t) for t in block_tables()]
    vmem = pl.BlockSpec(memory_space=pltpu.VMEM)
    hbm = pl.BlockSpec(memory_space=pl.ANY)
    return pl.pallas_call(
        wave_kernel,
        out_shape=(
            jax.ShapeDtypeStruct((2, W, W), BF16),
            jax.ShapeDtypeStruct((2, W, W), BF16),
            jax.ShapeDtypeStruct((4, 2, HALF, W), BF16),
            jax.ShapeDtypeStruct((4, 2, HALF, W), BF16),
        ),
        in_specs=[pl.BlockSpec(memory_space=pltpu.SMEM), vmem, vmem, vmem, vmem, hbm, hbm, vmem, vmem],
        out_specs=(vmem, vmem, hbm, hbm),
        scratch_shapes=[
            pltpu.VMEM((2, 4, 2 * W, 128), F32),
            pltpu.VMEM((2, W, W), F32),
            pltpu.VMEM((4, 256, W), BF16),
            pltpu.VMEM((4, 256, W), BF16),
            pltpu.VMEM((4, 256, W), F32),
            pltpu.VMEM((4, 256, W), F32),
            pltpu.VMEM((4, W, 256), BF16),
            pltpu.VMEM((4, W, 256), BF16),
            pltpu.VMEM((4, 4, W, 256), F32),
            pltpu.VMEM((4, 4, 256, W), BF16),
            pltpu.VMEM((4, 2, W, W), BF16),
            pltpu.VMEM((W, W), F32),
            pltpu.VMEM((4, 2, 2, HALF, W), BF16),
            pltpu.VMEM((2, W, W), F32),
            pltpu.SemaphoreType.DMA((4,)),
            pltpu.SemaphoreType.DMA,
            pltpu.SemaphoreType.DMA((8,)),
        ],
        compiler_params=pltpu.CompilerParams(vmem_limit_bytes=54 * MIB),
        cost_estimate=pl.CostEstimate(flops=20 * 10**9, bytes_accessed=20 * MIB, transcendentals=W * W),
        name="wave",
    )(info, own0, own1, below0, below1, probe, amp, *tables)


def second_kernel(starts_ref, up_ref, above_ref, out_ref):
    masks = []
    for block in range(4):
        lane = lane_index(block, 16)
        for source in range(2):
            start = starts_ref[source]
            masks.append(jnp.logical_and(lane < start, lane >= start - W))

    def body(rows):
        for part in range(2):
            for block in range(4):
                lanes = slice(block * 128, block * 128 + 128)
                own = jnp.where(masks[block * 2], up_ref[part, rows, lanes].astype(F32), 0.0)
                above = above_ref[part, rows, lanes].astype(F32)
                out_ref[part, rows, lanes] = own + jnp.where(masks[block * 2 + 1], above, 0.0)

    row_steps(out_ref.shape[1], 16, body, 2)


def first_kernel(starts_ref, up_ref, above_ref, left_ref, tile_ref, after_ref, out_ref):
    masks = [lane_index(block, 16) >= starts_ref[source] for block in range(4) for source in range(2)]

    def body(rows):
        for part in range(2):
            for block in range(4):
                lanes = slice(block * 128, block * 128 + 128)
                own = jnp.where(masks[block * 2], up_ref[part, rows, lanes].astype(F32), 0.0)
                above = jnp.where(masks[block * 2 + 1], above_ref[part, rows, lanes].astype(F32), 0.0)
                out_ref[part, rows, lanes] = own + above + left_ref[part, rows, lanes].astype(F32)

    row_steps(out_ref.shape[1], 16, body, 2)


def finish(starts, up, above, left, after):
    size = 128
    smem = pl.BlockSpec(memory_space=pltpu.SMEM)
    part = pl.BlockSpec((2, size, W), lambda i: (0, i, 0))
    keep = pl.BlockSpec(memory_space=pl.ANY)
    call = functools.partial(
        pl.pallas_call,
        grid=(W // size,),
        out_shape=jax.ShapeDtypeStruct((2, W, 2 * W), F32),
        compiler_params=pltpu.CompilerParams(vmem_limit_bytes=16 * MIB),
        cost_estimate=pl.CostEstimate(flops=4 * MIB, bytes_accessed=8 * MIB, transcendentals=0),
    )
    tile = call(
        second_kernel,
        in_specs=[smem, part, part],
        out_specs=pl.BlockSpec((2, size, W), lambda i: (0, i, 1)),
        name="second_half",
    )(starts, up, above)
    return call(
        first_kernel,
        in_specs=[smem, part, part, part, keep, keep],
        out_specs=part,
        input_output_aliases={4: 0},
        name="first_half",
    )(starts, up, above, left, tile, after)


def chip_sum_kernel(keep_ref, got_ref, out_ref):
    upper = lax.broadcasted_iota(jnp.int32, (8, W), 0) < 4

    def body(rows):
        short = pl.ds(pl.multiple_of(rows.start // 4, 16), 16)
        for mode in range(4):
            for part in range(2):
                total = keep_ref[mode, part, rows, :].astype(F32) + got_ref[mode, part, rows, :].astype(F32)
                pieces = [total[k * 8 : k * 8 + 8] for k in range(8)]
                turned = [pltpu.roll(piece, 4, 0) for piece in pieces]
                for x in range(4):
                    group = []
                    for k in (x // 2, x // 2 + 4):
                        if x % 2 == 0:
                            group.append(jnp.where(upper, pieces[k], turned[k + 2]))
                        else:
                            group.append(jnp.where(upper, turned[k], pieces[k + 2]))
                    out_ref[x, mode, part, short, :] = jnp.concatenate(group, axis=0).astype(BF16)

    row_steps(keep_ref.shape[2], 64, body)


def chip_sum(keep, got):
    spec = pl.BlockSpec((4, 2, 64, W), lambda i: (0, 0, i, 0))
    return pl.pallas_call(
        chip_sum_kernel,
        grid=(4,),
        out_shape=jax.ShapeDtypeStruct((4, 4, 2, 64, W), BF16),
        in_specs=[spec, spec],
        out_specs=pl.BlockSpec((4, 4, 2, 16, W), lambda i: (0, 0, 0, i, 0)),
        compiler_params=pltpu.CompilerParams(vmem_limit_bytes=16 * MIB),
        cost_estimate=pl.CostEstimate(flops=WEIGHT, bytes_accessed=6 * MIB, transcendentals=0),
        name="chip_sum",
    )(keep, got)


def row_blocks_kernel(got_ref, out_ref):
    upper = lax.broadcasted_iota(jnp.int32, (8, W), 0) < 4

    def body(rows):
        totals = []
        for mode in range(4):
            for part in range(2):
                totals.append(sum(got_ref[k, mode, part, rows, :].astype(F32) for k in range(4)))
        for half in range(2):
            pieces = [total[half * 8 : half * 8 + 8] for total in totals]
            turned = [pltpu.roll(piece, 4, 0) for piece in pieces]
            for odd in range(2):
                group = []
                for k in range(0, 8, 2):
                    if odd:
                        group.append(jnp.where(upper, turned[k], pieces[k + 1]))
                    else:
                        group.append(jnp.where(upper, pieces[k], turned[k + 1]))
                place = rows.start // 4 + half * 2 + odd
                out_ref[place] = jnp.concatenate(group, axis=0).astype(BF16)

    row_steps(got_ref.shape[3], 16, body)


def row_blocks(got):
    vmem = pl.BlockSpec(memory_space=pltpu.VMEM)
    return pl.pallas_call(
        row_blocks_kernel,
        out_shape=jax.ShapeDtypeStruct((16, 32, W), BF16),
        in_specs=[vmem],
        out_specs=vmem,
        compiler_params=pltpu.CompilerParams(vmem_limit_bytes=16 * MIB),
        cost_estimate=pl.CostEstimate(flops=MIB, bytes_accessed=3 * MIB, transcendentals=0),
        name="row_blocks",
    )(got)


ROW = ("y", "z_hi")
COL = ("z_lo", "x", "core")


def last_sum_kernel(got_ref, out_ref):
    total = sum(got_ref[k].astype(F32) for k in range(got_ref.shape[0]))
    for mode in range(4):
        for part in range(2):
            start = (mode * 2 + part) * 4
            out_ref[mode, part] = total[start : start + 4]


def last_sum(got):
    vmem = pl.BlockSpec(memory_space=pltpu.VMEM)
    return pl.pallas_call(
        last_sum_kernel,
        out_shape=jax.ShapeDtypeStruct((4, 2, 4, W), F32),
        in_specs=[vmem],
        out_specs=vmem,
        compiler_params=pltpu.CompilerParams(vmem_limit_bytes=16 * MIB),
        cost_estimate=pl.CostEstimate(flops=MIB, bytes_accessed=MIB, transcendentals=0),
        name="last_sum",
    )(got)


def chips_sum(send, keep):
    got = lax.ppermute(send, "core", [(0, 1), (1, 0)])
    blocks = chip_sum(keep, got)
    return blocks, lax.all_to_all(blocks, "x", 0, 0, tiled=True)


def rows_sum(blocks):
    got = lax.all_to_all(blocks, ("y", "z_hi", "z_lo"), 0, 0, tiled=True)
    return last_sum(got)


def per_device(object_field, probe_modes, positions, amplitudes, live_slots):
    row, col = lax.axis_index(ROW), lax.axis_index(COL)
    tile_rows, tile_cols = object_field.shape[1:]
    to_left = [(i + 1, i) for i in range(15)]
    to_right = [(i, i + 1) for i in range(15)]
    to_upper = [(i + 1, i) for i in range(7)]
    to_lower = [(i, i + 1) for i in range(7)]
    upper = lax.ppermute(positions, ROW, to_lower)
    right = [lax.ppermute(left_columns(object_field, h, HALF), COL, to_left) for h in range(2)]
    anchor = jnp.reshape(col * tile_cols, (1,)).astype(jnp.int32)
    chosen = [cut_columns(upper, anchor, object_field, right[h], h) for h in range(2)]
    below = [lax.ppermute(chosen[h], ROW, to_upper) for h in range(2)]
    positions, upper, live_slots, chosen[1] = lax.optimization_barrier(
        (positions, upper, live_slots, chosen[1])
    )
    own_start = positions[:, 1] - col * tile_cols
    upper_start = jnp.clip(upper[:, 1] - col * tile_cols, 0, tile_cols - 1)
    row_start = positions[0, 0] - row * tile_rows
    own = [cut_columns(positions, anchor, object_field, right[h], h) for h in range(2)]
    amp = amplitude_parts(amplitudes[0], chosen[1])
    info = jnp.stack([row_start, lax.axis_index("core"), live_slots[0], own_start[0]]).astype(jnp.int32)
    up, low, send, keep = wave(info, *own, *below, probe_modes, amp)
    above = lax.ppermute(low, ROW, to_lower)
    chip_terms, chips_terms = chips_sum(send, keep)
    starts = jnp.concatenate([own_start, upper_start])
    over = overflow(own_start[0], up, upper_start[0], above)
    left = lax.ppermute(over, COL, to_right)
    row_terms = row_blocks(chips_terms)
    probe_grad = rows_sum(row_terms)
    return finish(starts, up, above, left, row_terms), probe_grad


def solution(mesh):
    chips = jax.sharding.Mesh(mesh.devices.reshape(4, 2, 2, 4, 2), ROW + COL)
    slots = ROW + COL
    placed = (P(None, ROW, COL), P(), P(slots, None), P(slots, None, None), P(slots))
    return jax.shard_map(
        per_device,
        mesh=chips,
        in_specs=placed,
        out_specs=(P(None, ROW, COL), P(None, None, slots, None)),
        check_vma=False,
    )
```

```python
import functools
import math

import jax
import jax.numpy as jnp
import ml_dtypes
import numpy as np
from jax import lax
from jax.experimental import pallas as pl
from jax.experimental.pallas import tpu as pltpu
from jax.sharding import PartitionSpec as P

W = 512
Q = W // 4
HALF = W // 2
WEIGHT = 100 * 10**9
MIB = 1024 * 1024
F32 = jnp.float32
BF16 = jnp.bfloat16


def block_tables():
    step = np.arange(W).astype(np.float32) * np.float32(2.0 * math.pi / W)
    scale = np.float32(1.0 / math.sqrt(W))
    cos_of = (np.cos(step) * scale).astype(ml_dtypes.bfloat16).astype(np.float32)
    sin_of = (np.sin(step) * scale).astype(ml_dtypes.bfloat16).astype(np.float32)
    short = np.arange(Q)
    forward = []
    for part in range(4):
        phase = np.outer(4 * short + part, short) % W
        c, s = cos_of[phase], sin_of[phase]
        forward.append(np.block([[c, s], [-s, c]]))
    forward = np.stack(forward).astype(ml_dtypes.bfloat16)
    return forward, np.ascontiguousarray(forward.transpose(0, 2, 1))


def fold(parts, sign):
    (ar, ai), (br, bi), (cr, ci), (dr, di) = parts
    pr, pi, mr, mi = ar + cr, ai + ci, ar - cr, ai - ci
    qr, qi, nr, ni = br + dr, bi + di, br - dr, bi - di
    if sign < 0:
        nr, ni = -nr, -ni
    return (
        (pr + qr, pi + qi),
        (mr + ni, mi - nr),
        (pr - qr, pi - qi),
        (mr - ni, mi + nr),
    )


def dot(a, b):
    return jnp.dot(a, b, preferred_element_type=F32)


def amplitude_kernel(amp_ref, pick_ref, after_ref, out_ref, sorted_ref):
    rows = amp_ref[...]
    high = rows.astype(BF16)
    rest = rows - high.astype(F32)
    middle = rest.astype(BF16)
    low = (rest - middle.astype(F32)).astype(BF16)
    for c in range(4):
        pick = pick_ref[:, c * Q : (c + 1) * Q]
        sorted_ref[c] = (dot(high, pick) + dot(middle, pick)) + dot(low, pick)
    for c in range(4):
        for r in range(4):
            out_ref[r * Q : (r + 1) * Q, c * Q : (c + 1) * Q] = sorted_ref[c, pl.ds(r, Q, stride=4), :]


def amplitude_parts(amp, after):
    source = np.arange(W)
    pick = np.zeros((W, W), ml_dtypes.bfloat16)
    pick[source, (source % 4) * Q + source // 4] = 1
    return pl.pallas_call(
        amplitude_kernel,
        out_shape=jax.ShapeDtypeStruct((W, W), F32),
        in_specs=[pl.BlockSpec(memory_space=pltpu.VMEM)] * 2 + [pl.BlockSpec(memory_space=pl.ANY)],
        scratch_shapes=[pltpu.VMEM((4, W, Q), F32)],
        compiler_params=pltpu.CompilerParams(vmem_limit_bytes=16 * MIB),
        cost_estimate=pl.CostEstimate(flops=6 * W**3, bytes_accessed=3 * MIB, transcendentals=0),
        name="amplitude_parts",
    )(amp, jnp.asarray(pick), after)


def overflow(own_start, up, upper_start, above):
    lane = lax.broadcasted_iota(jnp.int32, up.shape, 2)
    own = jnp.where(lane < own_start - W, up.astype(F32), 0.0)
    return (own + jnp.where(lane < upper_start - W, above.astype(F32), 0.0)).astype(BF16)


def lane_index(block, rows):
    return lax.broadcasted_iota(jnp.int32, (rows, 128), 1) + block * 128


def row_steps(count, size, body, unroll=1):
    def step_of(step, carry):
        body(pl.ds(pl.multiple_of(step * size, size), size))
        return carry

    lax.fori_loop(0, count // size, step_of, 0, unroll=unroll)


def columns_kernel(corner_ref, anchor_ref, tile_ref, right_ref, out_ref):
    start = jnp.clip(corner_ref[0, 1] - anchor_ref[0], 0, 2 * W - 1)
    masks = [(lane_index(k, 16) >= start, lane_index(k, 16) >= start - W) for k in range(4)]

    def body(rows):
        for part in range(2):
            for k, (in_first, in_second) in enumerate(masks):
                lanes = slice(k * 128, k * 128 + 128)
                first = tile_ref[part, rows, lanes].astype(F32)
                second = tile_ref[part, rows, W + k * 128 : W + k * 128 + 128].astype(F32)
                beyond = right_ref[part, rows, lanes].astype(F32)
                value = jnp.where(in_first, first, jnp.where(in_second, second, beyond))
                out_ref[part, rows, lanes] = value.astype(BF16)

    row_steps(out_ref.shape[1], 16, body, 2)


def cut_columns(corner, anchor, tile, right, chunk):
    rows = right.shape[1]
    whole = pl.BlockSpec((2, rows, W), lambda i: (0, 0, 0))
    return pl.pallas_call(
        columns_kernel,
        grid=(1,),
        out_shape=jax.ShapeDtypeStruct((2, rows, W), BF16),
        in_specs=[
            pl.BlockSpec(memory_space=pltpu.SMEM),
            pl.BlockSpec(memory_space=pltpu.SMEM),
            pl.BlockSpec((2, rows, 2 * W), lambda i: (0, chunk, 0)),
            whole,
        ],
        out_specs=whole,
        compiler_params=pltpu.CompilerParams(vmem_limit_bytes=16 * MIB),
        cost_estimate=pl.CostEstimate(flops=WEIGHT, bytes_accessed=2 * MIB, transcendentals=0),
        name="cut_columns",
    )(corner, anchor, tile, right)


def copy_kernel(tile_ref, out_ref):
    out_ref[...] = tile_ref[...]


def left_columns(tile, chunk, rows):
    return pl.pallas_call(
        copy_kernel,
        grid=(1,),
        out_shape=jax.ShapeDtypeStruct((2, rows, W), BF16),
        in_specs=[pl.BlockSpec((2, rows, W), lambda i: (0, chunk, 0))],
        out_specs=pl.BlockSpec((2, rows, W), lambda i: (0, 0, 0)),
        compiler_params=pltpu.CompilerParams(vmem_limit_bytes=16 * MIB),
        cost_estimate=pl.CostEstimate(flops=0, bytes_accessed=MIB, transcendentals=0),
        name="left_columns",
    )(tile)


def wave_kernel(
    info_ref, own0_ref, own1_ref, below0_ref, below1_ref, probe_hbm, amp_hbm, forward_ref, adjoint_ref,
    up_ref, low_ref, send_hbm, keep_hbm,
    tall, patch, folded0, folded1, mid0, mid1, wide0, wide1, far, waves, probe, amp, terms_out, object_sum,
    probe_sem, amp_sem, out_sem,
):
    row_start = info_ref[0]
    core = info_ref[1]
    live = info_ref[2].astype(F32)
    col_start = info_ref[3]
    turn_block, turn = col_start % W // 128, col_start % 128
    folded, mid, wide = (folded0, folded1), (mid0, mid1), (wide0, wide1)

    def loop(count, body, unroll=1):
        lax.fori_loop(0, count, lambda i, c: (body(i), c)[1], 0, unroll=unroll)

    def rows16(step, base=0):
        if isinstance(step, int):
            return slice(base + step * 16, base + step * 16 + 16)
        return pl.ds(pl.multiple_of(base + step * 16, 16), 16)

    def probe_copy(m):
        return pltpu.make_async_copy(probe_hbm.at[m], probe.at[m], probe_sem.at[m])

    def send_copy(m):
        return pltpu.make_async_copy(terms_out.at[m, 1 - core], send_hbm.at[m], out_sem.at[m])

    def keep_copy(m):
        return pltpu.make_async_copy(terms_out.at[m, core], keep_hbm.at[m], out_sem.at[4 + m])

    amp_copy = pltpu.make_async_copy(amp_hbm, amp, amp_sem)
    for m in range(4):
        probe_copy(m).start()
    amp_copy.start()

    blocks = [slice(k * 128, (k + 1) * 128) for k in range(4)]
    lane_blocks = [(part, k, blocks[k]) for part in range(2) for k in range(4)]

    def stack_rows(step):
        for part, k, lanes in lane_blocks:
            for h, ref in enumerate((own0_ref, own1_ref, below0_ref, below1_ref)):
                tall[part, k, rows16(step, h * HALF), :] = ref[part, rows16(step), lanes].astype(F32)

    loop(HALF // 16, stack_rows, 2)
    lane16 = lax.broadcasted_iota(jnp.int32, (16, 128), 1)

    def take_rows(step):
        for part in range(2):
            turned = []
            for k in range(4):
                value = tall[part, (turn_block + k) % 4, pl.ds(row_start + step * 16, 16), :]
                turned.append(pltpu.roll(value, (128 - turn) % 128, 1))
            for k, lanes in enumerate(blocks):
                value = jnp.where(lane16 < 128 - turn, turned[k], turned[(k + 1) % 4])
                patch[part, rows16(step), lanes] = value

    loop(W // 16, take_rows, 4)

    def exit_fold(m, quarter):
        for step in (quarter * 2, quarter * 2 + 1):
            for lanes in blocks:
                parts = []
                for q in range(4):
                    rows = rows16(step, q * Q)
                    pr = probe[m, 0, rows, lanes].astype(F32)
                    pi = probe[m, 1, rows, lanes].astype(F32)
                    xr, xi = patch[0, rows, lanes], patch[1, rows, lanes]
                    er = (pr * xr - pi * xi).astype(BF16).astype(F32)
                    ei = (pr * xi + pi * xr).astype(BF16).astype(F32)
                    parts.append((er, ei))
                for r, (zr, zi) in enumerate(fold(parts, 1)):
                    folded[m % 2][r, rows16(step), lanes] = zr.astype(BF16)
                    folded[m % 2][r, rows16(step, Q), lanes] = zi.astype(BF16)

    def column_fold(m, r):
        for step in range(Q // 16):
            parts = []
            for lanes in blocks:
                yr = mid[m % 2][r, rows16(step), lanes].astype(BF16).astype(F32)
                yi = mid[m % 2][r, rows16(step, Q), lanes].astype(BF16).astype(F32)
                parts.append((yr, yi))
            for c, (wr, wi) in enumerate(fold(parts, 1)):
                wide[m % 2][c, rows16(step, r * Q), 0:128] = wr.astype(BF16)
                wide[m % 2][c, rows16(step, r * Q), 128:256] = wi.astype(BF16)

    def forward_step(tick, i):
        if tick < 4:
            exit_fold(tick, i)
        if 0 <= tick - 1 < 4:
            mid[(tick - 1) % 2][i] = dot(forward_ref[i], folded[(tick - 1) % 2][i])
        if 0 <= tick - 2 < 4:
            column_fold(tick - 2, i)
        if 0 <= tick - 3 < 4:
            far[tick - 3, i] = dot(wide[(tick - 3) % 2][i], adjoint_ref[i])

    for tick in range(7):
        if tick < 4:
            probe_copy(tick).wait()
        [forward_step(tick, i) for i in range(4)]

    amp_copy.wait()

    def residual(step):
        r, inner = step // 8, step % 8
        rows = rows16(step)
        for c, lanes in enumerate(blocks):
            fields = [(far[m, c, rows, 0:128], far[m, c, rows, 128:256]) for m in range(4)]
            intensity = sum(fr * fr + fi * fi for fr, fi in fields)
            ratio = live * (1.0 - amp[rows, lanes] * lax.rsqrt(jnp.maximum(intensity, 0.25)))
            for m, (fr, fi) in enumerate(fields):
                waves[m, r, rows16(inner), lanes] = (fr * ratio).astype(BF16)
                waves[m, r, rows16(inner, Q), lanes] = (fi * ratio).astype(BF16)

    loop(W // 16, residual, 2)

    def row_unfold(m, c):
        lanes = blocks[c]
        for step in range(Q // 16):
            parts = [
                (mid[m % 2][r, rows16(step), lanes], mid[m % 2][r, rows16(step, Q), lanes])
                for r in range(4)
            ]
            for q, (yr, yi) in enumerate(fold(parts, -1)):
                wide[m % 2][c, rows16(step, q * Q), 0:128] = yr.astype(BF16)
                wide[m % 2][c, rows16(step, q * Q), 128:256] = yi.astype(BF16)

    upper8 = lax.broadcasted_iota(jnp.int32, (8, 128), 0) < 4

    def by_core(value):
        pieces = [value[k * 8 : k * 8 + 8] for k in range(4)]
        turned = [pltpu.roll(piece, 4, 0) for piece in pieces]
        first = [jnp.where(upper8, pieces[k], turned[k + 1]) for k in (0, 2)]
        second = [jnp.where(upper8, turned[k], pieces[k + 1]) for k in (0, 2)]
        return [jnp.concatenate(half, axis=0).astype(BF16) for half in (first, second)]

    def terms(m, quarter):
        for step in range(4):
            start = quarter * 128 + step * 32
            rows, short = slice(start, start + 32), slice(start // 2, start // 2 + 16)
            parts = [(far[m, c, rows, 0:128], far[m, c, rows, 128:256]) for c in range(4)]
            for lanes, (gr, gi) in zip(blocks, fold(parts, -1)):
                pr = probe[m, 0, rows, lanes].astype(F32)
                pi = probe[m, 1, rows, lanes].astype(F32)
                object_r, object_i = pr * gr + pi * gi, pr * gi - pi * gr
                if m:
                    object_r = object_r + object_sum[0, rows, lanes]
                    object_i = object_i + object_sum[1, rows, lanes]
                object_sum[0, rows, lanes] = object_r
                object_sum[1, rows, lanes] = object_i
                xr, xi = patch[0, rows, lanes], patch[1, rows, lanes]
                for part, term in enumerate((xr * gr + xi * gi, xr * gi - xi * gr)):
                    for half, value in enumerate(by_core(term)):
                        terms_out[m, half, part, short, lanes] = value

    def adjoint_step(tick, i):
        if tick < 4:
            mid[tick % 2][i] = dot(adjoint_ref[i], waves[tick, i])
        if 0 <= tick - 1 < 4:
            row_unfold(tick - 1, i)
        if 0 <= tick - 2 < 4:
            far[tick - 2, i] = dot(wide[(tick - 2) % 2][i], forward_ref[i])
        if 0 <= tick - 3 < 4:
            terms(tick - 3, i)

    for tick in range(7):
        [adjoint_step(tick, i) for i in range(4)]
        if tick >= 3:
            send_copy(tick - 3).start()
            keep_copy(tick - 3).start()

    def clear(step):
        for part, k, lanes in lane_blocks:
            tall[part, k, rows16(step), :] = jnp.zeros((16, 128), F32)
            tall[part, k, rows16(step, W), :] = jnp.zeros((16, 128), F32)

    loop(W // 16, clear, 2)

    def put_rows(step):
        for part in range(2):
            turned = [pltpu.roll(object_sum[part, rows16(step), lanes], turn, 1) for lanes in blocks]
            for k in range(4):
                value = jnp.where(lane16 < turn, turned[(k + 3) % 4], turned[k])
                tall[part, (turn_block + k) % 4, pl.ds(row_start + step * 16, 16), :] = value

    loop(W // 16, put_rows, 4)

    def split_rows(step):
        rows = rows16(step)
        for part, k, lanes in lane_blocks:
            up_ref[part, rows, lanes] = tall[part, k, rows, :].astype(BF16)
            low_ref[part, rows, lanes] = tall[part, k, rows16(step, W), :].astype(BF16)

    loop(W // 16, split_rows, 2)
    for m in range(4):
        send_copy(m).wait()
        keep_copy(m).wait()


def wave(info, own0, own1, below0, below1, probe, amp):
    tables = [jnp.asarray(t) for t in block_tables()]
    vmem = pl.BlockSpec(memory_space=pltpu.VMEM)
    hbm = pl.BlockSpec(memory_space=pl.ANY)
    return pl.pallas_call(
        wave_kernel,
        out_shape=(
            jax.ShapeDtypeStruct((2, W, W), BF16),
            jax.ShapeDtypeStruct((2, W, W), BF16),
            jax.ShapeDtypeStruct((4, 2, HALF, W), BF16),
            jax.ShapeDtypeStruct((4, 2, HALF, W), BF16),
        ),
        in_specs=[pl.BlockSpec(memory_space=pltpu.SMEM), vmem, vmem, vmem, vmem, hbm, hbm, vmem, vmem],
        out_specs=(vmem, vmem, hbm, hbm),
        scratch_shapes=[
            pltpu.VMEM((2, 4, 2 * W, 128), F32),
            pltpu.VMEM((2, W, W), F32),
            pltpu.VMEM((4, 256, W), BF16),
            pltpu.VMEM((4, 256, W), BF16),
            pltpu.VMEM((4, 256, W), F32),
            pltpu.VMEM((4, 256, W), F32),
            pltpu.VMEM((4, W, 256), BF16),
            pltpu.VMEM((4, W, 256), BF16),
            pltpu.VMEM((4, 4, W, 256), F32),
            pltpu.VMEM((4, 4, 256, W), BF16),
            pltpu.VMEM((4, 2, W, W), BF16),
            pltpu.VMEM((W, W), F32),
            pltpu.VMEM((4, 2, 2, HALF, W), BF16),
            pltpu.VMEM((2, W, W), F32),
            pltpu.SemaphoreType.DMA((4,)),
            pltpu.SemaphoreType.DMA,
            pltpu.SemaphoreType.DMA((8,)),
        ],
        compiler_params=pltpu.CompilerParams(vmem_limit_bytes=54 * MIB),
        cost_estimate=pl.CostEstimate(flops=20 * 10**9, bytes_accessed=20 * MIB, transcendentals=W * W),
        name="wave",
    )(info, own0, own1, below0, below1, probe, amp, *tables)


def second_kernel(starts_ref, up_ref, above_ref, out_ref):
    masks = []
    for block in range(4):
        lane = lane_index(block, 16)
        for source in range(2):
            start = starts_ref[source]
            masks.append(jnp.logical_and(lane < start, lane >= start - W))

    def body(rows):
        for part in range(2):
            for block in range(4):
                lanes = slice(block * 128, block * 128 + 128)
                own = jnp.where(masks[block * 2], up_ref[part, rows, lanes].astype(F32), 0.0)
                above = above_ref[part, rows, lanes].astype(F32)
                out_ref[part, rows, lanes] = own + jnp.where(masks[block * 2 + 1], above, 0.0)

    row_steps(out_ref.shape[1], 16, body, 2)


def first_kernel(starts_ref, up_ref, above_ref, left_ref, tile_ref, after_ref, out_ref):
    masks = [lane_index(block, 16) >= starts_ref[source] for block in range(4) for source in range(2)]

    def body(rows):
        for part in range(2):
            for block in range(4):
                lanes = slice(block * 128, block * 128 + 128)
                own = jnp.where(masks[block * 2], up_ref[part, rows, lanes].astype(F32), 0.0)
                above = jnp.where(masks[block * 2 + 1], above_ref[part, rows, lanes].astype(F32), 0.0)
                out_ref[part, rows, lanes] = own + above + left_ref[part, rows, lanes].astype(F32)

    row_steps(out_ref.shape[1], 16, body, 2)


PART = pl.BlockSpec((2, 128, W), lambda i: (0, i, 0))


def tile_call(kernel, **options):
    return pl.pallas_call(
        kernel,
        grid=(4,),
        out_shape=jax.ShapeDtypeStruct((2, W, 2 * W), F32),
        compiler_params=pltpu.CompilerParams(vmem_limit_bytes=16 * MIB),
        cost_estimate=pl.CostEstimate(flops=4 * MIB, bytes_accessed=8 * MIB, transcendentals=0),
        **options,
    )


def second_half(starts, up, above):
    return tile_call(
        second_kernel,
        in_specs=[pl.BlockSpec(memory_space=pltpu.SMEM), PART, PART],
        out_specs=pl.BlockSpec((2, 128, W), lambda i: (0, i, 1)),
        name="second_half",
    )(starts, up, above)


def first_half(starts, up, above, left, tile, after):
    keep = pl.BlockSpec(memory_space=pl.ANY)
    return tile_call(
        first_kernel,
        in_specs=[pl.BlockSpec(memory_space=pltpu.SMEM), PART, PART, PART, keep, keep],
        out_specs=PART,
        input_output_aliases={4: 0},
        name="first_half",
    )(starts, up, above, left, tile, after)


def chip_sum_kernel(keep_ref, got_ref, out_ref):
    upper = lax.broadcasted_iota(jnp.int32, (8, W), 0) < 4

    def body(rows):
        short = pl.ds(pl.multiple_of(rows.start // 4, 16), 16)
        for mode in range(4):
            for part in range(2):
                total = keep_ref[mode, part, rows, :].astype(F32) + got_ref[mode, part, rows, :].astype(F32)
                pieces = [total[k * 8 : k * 8 + 8] for k in range(8)]
                turned = [pltpu.roll(piece, 4, 0) for piece in pieces]
                for x in range(4):
                    group = []
                    for k in (x // 2, x // 2 + 4):
                        if x % 2 == 0:
                            group.append(jnp.where(upper, pieces[k], turned[k + 2]))
                        else:
                            group.append(jnp.where(upper, turned[k], pieces[k + 2]))
                    out_ref[x, mode, part, short, :] = jnp.concatenate(group, axis=0).astype(BF16)

    row_steps(keep_ref.shape[2], 64, body)


def chip_sum(keep, got):
    spec = pl.BlockSpec((4, 2, 64, W), lambda i: (0, 0, i, 0))
    return pl.pallas_call(
        chip_sum_kernel,
        grid=(4,),
        out_shape=jax.ShapeDtypeStruct((4, 4, 2, 64, W), BF16),
        in_specs=[spec, spec],
        out_specs=pl.BlockSpec((4, 4, 2, 16, W), lambda i: (0, 0, 0, i, 0)),
        compiler_params=pltpu.CompilerParams(vmem_limit_bytes=16 * MIB),
        cost_estimate=pl.CostEstimate(flops=WEIGHT, bytes_accessed=6 * MIB, transcendentals=0),
        name="chip_sum",
    )(keep, got)


def row_blocks_kernel(got_ref, out_ref):
    upper = lax.broadcasted_iota(jnp.int32, (8, W), 0) < 4

    def body(rows):
        totals = []
        for mode in range(4):
            for part in range(2):
                totals.append(sum(got_ref[k, mode, part, rows, :].astype(F32) for k in range(4)))
        for half in range(2):
            pieces = [total[half * 8 : half * 8 + 8] for total in totals]
            turned = [pltpu.roll(piece, 4, 0) for piece in pieces]
            for odd in range(2):
                group = []
                for k in range(0, 8, 2):
                    if odd:
                        group.append(jnp.where(upper, turned[k], pieces[k + 1]))
                    else:
                        group.append(jnp.where(upper, pieces[k], turned[k + 1]))
                place = rows.start // 4 + half * 2 + odd
                out_ref[place] = jnp.concatenate(group, axis=0).astype(BF16)

    row_steps(got_ref.shape[3], 16, body)


def row_blocks(got):
    vmem = pl.BlockSpec(memory_space=pltpu.VMEM)
    return pl.pallas_call(
        row_blocks_kernel,
        out_shape=jax.ShapeDtypeStruct((16, 32, W), BF16),
        in_specs=[vmem],
        out_specs=vmem,
        compiler_params=pltpu.CompilerParams(vmem_limit_bytes=16 * MIB),
        cost_estimate=pl.CostEstimate(flops=MIB, bytes_accessed=3 * MIB, transcendentals=0),
        name="row_blocks",
    )(got)


ROW = ("y", "z_hi")
COL = ("z_lo", "x", "core")


def last_sum_kernel(got_ref, out_ref):
    total = sum(got_ref[k].astype(F32) for k in range(got_ref.shape[0]))
    for mode in range(4):
        for part in range(2):
            start = (mode * 2 + part) * 4
            out_ref[mode, part] = total[start : start + 4]


def last_sum(got):
    vmem = pl.BlockSpec(memory_space=pltpu.VMEM)
    return pl.pallas_call(
        last_sum_kernel,
        out_shape=jax.ShapeDtypeStruct((4, 2, 4, W), F32),
        in_specs=[vmem],
        out_specs=vmem,
        compiler_params=pltpu.CompilerParams(vmem_limit_bytes=16 * MIB),
        cost_estimate=pl.CostEstimate(flops=MIB, bytes_accessed=MIB, transcendentals=0),
        name="last_sum",
    )(got)


def chips_sum(send, keep):
    got = lax.ppermute(send, "core", [(0, 1), (1, 0)])
    blocks = chip_sum(keep, got)
    return blocks, lax.all_to_all(blocks, "x", 0, 0, tiled=True)


def rows_sum(blocks):
    got = lax.all_to_all(blocks, ("y", "z_hi", "z_lo"), 0, 0, tiled=True)
    return last_sum(got)


def per_device(object_field, probe_modes, positions, amplitudes, live_slots):
    row, col = lax.axis_index(ROW), lax.axis_index(COL)
    tile_rows, tile_cols = object_field.shape[1:]
    to_left = [(i + 1, i) for i in range(15)]
    to_right = [(i, i + 1) for i in range(15)]
    to_upper = [(i + 1, i) for i in range(7)]
    to_lower = [(i, i + 1) for i in range(7)]
    upper = lax.ppermute(positions, ROW, to_lower)
    right = [lax.ppermute(left_columns(object_field, h, HALF), COL, to_left) for h in range(2)]
    anchor = jnp.reshape(col * tile_cols, (1,)).astype(jnp.int32)
    chosen = [cut_columns(upper, anchor, object_field, right[h], h) for h in range(2)]
    below = [lax.ppermute(chosen[h], ROW, to_upper) for h in range(2)]
    positions, upper, live_slots, chosen[1] = lax.optimization_barrier(
        (positions, upper, live_slots, chosen[1])
    )
    own_start = positions[:, 1] - col * tile_cols
    upper_start = jnp.clip(upper[:, 1] - col * tile_cols, 0, tile_cols - 1)
    row_start = positions[0, 0] - row * tile_rows
    own = [cut_columns(positions, anchor, object_field, right[h], h) for h in range(2)]
    amp = amplitude_parts(amplitudes[0], chosen[1])
    info = jnp.stack([row_start, lax.axis_index("core"), live_slots[0], own_start[0]]).astype(jnp.int32)
    up, low, send, keep = wave(info, *own, *below, probe_modes, amp)
    above = lax.ppermute(low, ROW, to_lower)
    chip_terms, chips_terms = chips_sum(send, keep)
    starts = jnp.concatenate([own_start, upper_start])
    over = overflow(own_start[0], up, upper_start[0], above)
    left = lax.ppermute(over, COL, to_right)
    tile = second_half(starts, up, above)
    chips_terms, tile = lax.optimization_barrier((chips_terms, tile))
    row_terms = row_blocks(chips_terms)
    probe_grad = rows_sum(row_terms)
    return first_half(starts, up, above, left, tile, row_terms), probe_grad


def solution(mesh):
    chips = jax.sharding.Mesh(mesh.devices.reshape(4, 2, 2, 4, 2), ROW + COL)
    slots = ROW + COL
    placed = (P(None, ROW, COL), P(), P(slots, None), P(slots, None, None), P(slots))
    return jax.shard_map(
        per_device,
        mesh=chips,
        in_specs=placed,
        out_specs=(P(None, ROW, COL), P(None, None, slots, None)),
        check_vma=False,
    )
```
